512 devices in a mesh: dp: 8 (over z_hi, core), latent: 64 (over z_lo, y, x).
Axes of the slice: x: 4, y: 8, z: 8 (z_hi: 4, z_lo: 2; z = z_hi * 2 + z_lo), core: 2. Of those that a mesh axis runs over, the one named last changes fastest.
Arguments:
- residual: bfloat16 [1536, 4608], P(('dp', 'latent')), may hold values from -6 to 6
- errors: bfloat16 [1536, 4608], P(('dp', 'latent')), may hold values from -192 to 192
- enc_weight: bfloat16 [4608, 8192], P(None, 'latent'), may hold values from -0.09375 to 0.09375
- dec_weight: bfloat16 [8192, 4608], P('latent'), may hold values from -0.09375 to 0.09375
- dead_mask: int32 [8192], P('latent'), may hold values from 0 to 1, as said below
Outputs:
- enc_grad: bfloat16 [4608, 8192], P(None, 'latent')
- dec_grad: bfloat16 [8192, 4608], P('latent')
The draws below stay inside these ranges and needn't reach their ends.
Inputs may be any that keep to these rules, and one draw needn't show every extreme that they name: `dead_mask`: in each aligned block of 128 latents (the latents of one device) at most 64 are dead, and some block has exactly 64 dead latents.
All inputs are finite; a program needn't handle non-finite values.
Results may differ from the reference program's by a relative error of at most 0.017.
Values may be sent and summed in bfloat16 or wider, within the bound.
A program may use at most 64 MiB of HBM per device.

```python
import math
import jax
import jax.numpy as jnp
from jax import lax

D = 4608
LAT_DEV = 128
DEAD_DEV = 64
GROUP_ROWS = 192
TOKENS = 1536
LATENTS = 8192
N_DP = 8


def draw_errors(key, part):
    key = jax.random.fold_in(key, 11)
    key_rows, key_cols, key_vals = jax.random.split(key, 3)
    col_ramp = jnp.exp(jnp.arange(D, dtype=jnp.float32) * (math.log(10.0) / D)) / math.sqrt(10.0)
    row_scale = jnp.exp(jax.random.uniform(key_rows, (TOKENS, 1), jnp.float32, math.log(0.3), math.log(3.0)))
    col_scale = jnp.exp(jax.random.uniform(key_cols, (1, D), jnp.float32, math.log(0.5), math.log(2.0)))
    values = jax.random.normal(key_vals, (TOKENS, D), jnp.float32) * row_scale * col_scale * col_ramp
    return values.astype(jnp.bfloat16)


def block_perm(block_key):
    return jax.random.permutation(block_key, LAT_DEV)


def draw_dead_mask(key, part):
    key = jax.random.fold_in(key, 23)
    key_base, key_pick, key_heavy, key_top, key_perm = jax.random.split(key, 5)
    blocks = LATENTS // LAT_DEV
    base_counts = jax.random.randint(key_base, (blocks,), 2, DEAD_DEV // 3 + 1)
    is_heavy = jax.random.randint(key_pick, (blocks,), 0, 8) == 0
    high_counts = jax.random.randint(key_heavy, (blocks,), DEAD_DEV // 2, DEAD_DEV + 1)
    counts = jnp.where(is_heavy, high_counts, base_counts)
    top_block = jax.random.randint(key_top, (), 0, blocks)
    counts = jnp.where(jnp.arange(blocks) == top_block, DEAD_DEV, counts)
    rank_table = jax.vmap(block_perm)(jax.random.split(key_perm, blocks))
    return (rank_table < counts[:, None]).astype(jnp.int32).reshape(LATENTS)


def steps_of(stream_key, shape, shards, smallest, top_value):
    gain, own = 1.0, jax.random.fold_in(stream_key, 6)
    for axis_at, parts in shards:
        steps = jnp.exp(jax.random.uniform(jax.random.fold_in(own, axis_at), (parts,), jnp.float32, smallest / len(shards), top_value / len(shards)))
        gain = gain * jnp.repeat(steps, shape[axis_at] // parts).reshape([-1 if axis == axis_at else 1 for axis in range(len(shape))])
    return gain


def gaussian(key, extent, deviation, reach, pieces=(), held_as=jnp.bfloat16):
    loudness = steps_of(key, extent, pieces, -0.22, 0.18) if pieces else 1.0
    result = jax.random.normal(key, extent, jnp.float32) * deviation * loudness
    return jnp.minimum(jnp.maximum(result, -reach), reach).astype(held_as)


def setup_inputs(seed: int = 0) -> dict:
    keys = jax.random.split(jax.random.key(seed), 6)
    return {
        "residual": gaussian(keys[0], (TOKENS, D), 1.0, 6.0, ((0, 512),)),
        "errors": draw_errors(jax.random.fold_in(keys[5], 71), 0),
        "enc_weight": gaussian(keys[2], (D, LATENTS), D ** -0.5, 0.09375, ((1, 64),)),
        "dec_weight": gaussian(keys[3], (LATENTS, D), D ** -0.5, 0.09375, ((0, 64),)),
        "dead_mask": draw_dead_mask(jax.random.fold_in(keys[5], 71), 0),
    }


def reference(residual, errors, enc_weight, dec_weight, dead_mask):
    dead_cols = dead_mask.astype(jnp.float32)
    dec_full = dec_weight.astype(jnp.float32)
    pre_acts = jnp.dot(residual.astype(jnp.float32), enc_weight.astype(jnp.float32), preferred_element_type=jnp.float32)
    ghost_acts = jnp.exp(pre_acts) * dead_cols[None, :]
    acts_bf = ghost_acts.astype(jnp.bfloat16)
    ghost_out = jnp.dot(acts_bf.astype(jnp.float32), dec_full, preferred_element_type=jnp.float32)
    err_full = errors.astype(jnp.float32)
    err_rms = jnp.sqrt(lax.optimization_barrier(jnp.mean(err_full * err_full, axis=1, keepdims=True)) + 1e-06)
    ghost_rms = jnp.sqrt(lax.optimization_barrier(jnp.mean(ghost_out * ghost_out, axis=1, keepdims=True)) + 1e-06)
    norm_scale = err_rms / (2.0 * ghost_rms)
    grad_out = (norm_scale * (norm_scale * ghost_out - err_full) / err_rms).astype(jnp.bfloat16)
    back_grad = jnp.dot(grad_out.astype(jnp.float32), dec_full.T, preferred_element_type=jnp.float32)
    pre_grad = (back_grad * ghost_acts).astype(jnp.bfloat16)
    factor = 1.0 / math.sqrt(TOKENS)

    def add_group(totals, group_data):
        acts_group, grad_group, rows_group, pre_group = group_data
        dec_part = jnp.dot(acts_group.astype(jnp.float32).T, grad_group.astype(jnp.float32), preferred_element_type=jnp.float32) * factor
        enc_part = jnp.dot(rows_group.astype(jnp.float32).T, pre_group.astype(jnp.float32), preferred_element_type=jnp.float32) * factor
        dec_part = lax.optimization_barrier(dec_part.astype(jnp.bfloat16)).astype(jnp.float32)
        enc_part = lax.optimization_barrier(enc_part.astype(jnp.bfloat16)).astype(jnp.float32)
        return ((totals[0] + enc_part, totals[1] + dec_part), None)
    grouped = (acts_bf.reshape(N_DP, GROUP_ROWS, LATENTS), grad_out.reshape(N_DP, GROUP_ROWS, D), residual.reshape(N_DP, GROUP_ROWS, D), pre_grad.reshape(N_DP, GROUP_ROWS, LATENTS))
    start_sums = (jnp.zeros((D, LATENTS), jnp.float32), jnp.zeros((LATENTS, D), jnp.float32))
    (enc_sum, dec_sum), _ = lax.scan(add_group, start_sums, grouped)
    return (enc_sum.astype(jnp.bfloat16), dec_sum.astype(jnp.bfloat16))
```

```python
import math

import jax
import jax.numpy as jnp
from jax import lax
from jax.experimental import pallas as pl
from jax.experimental.pallas import tpu as pltpu
from jax.sharding import PartitionSpec as P

NX, NY, NZ = 4, 8, 8
DEAD = 64
Q = 4
SLAB = 16
EPS = 1e-06
MESH = pl.DeviceIdType.MESH
F32, BF16 = jnp.float32, jnp.bfloat16


def dot_nt(a, b):
    return lax.dot_general(a, b, (((1,), (1,)), ((), ())), preferred_element_type=F32)


def dot_nn(a, b):
    return lax.dot_general(a, b, (((1,), (0,)), ((), ())), preferred_element_type=F32)


def dot_tn(a, b):
    return lax.dot_general(a, b, (((0,), (0,)), ((), ())), preferred_element_type=F32)


def iota(shape, dim):
    return lax.broadcasted_iota(jnp.int32, shape, dim)


def sum_quads(v):
    n = v.shape[0]
    row = iota(v.shape, 0)
    v = v + jnp.where(row % 2 == 0, pltpu.roll(v, n - 1, 0), pltpu.roll(v, 1, 0))
    return v + jnp.where(row % 4 < 2, pltpu.roll(v, n - 2, 0), pltpu.roll(v, 2, 0))


def fold(prod):
    same = iota(prod.shape, 0) % Q == iota(prod.shape, 1) // DEAD
    prod = jnp.where(same, prod, 0.0)
    half = 2 * DEAD
    pair = prod[:, :half] + prod[:, half:]
    return sum_quads(pair + pltpu.roll(pair, DEAD, 1))


def unfold(vals):
    wide = jnp.concatenate([vals, vals], axis=1)
    row = iota(wide.shape, 0)
    keep = (row % Q == iota(wide.shape, 1) // DEAD) & (row % SLAB < 3 * Q)
    return jnp.where(keep, wide, 0.0).astype(BF16)


def to_slab(ref, width):
    rows = iota((SLAB, width), 0)
    out = jnp.zeros((SLAB, width), F32)
    for r in range(3):
        for q in range(Q):
            piece = ref[r : r + 1, q * width : (q + 1) * width].astype(F32)
            out = jnp.where(rows == Q * r + q, piece, out)
    return out


def kernel(
    res_ref, err_ref, enc_ref, dec_ref, mask_ref,
    dgrad_ref, egrad_ref, pick_ref,
    e4, w4, rbuf, gbuf, obuf, osib, s1, xrecv, s2, yrecv, ghost, aexp, pexp, zsend, zrecv, zsum, zall,
    w_s, w_r, gy_s, gy_r, gx_s, gx_r, gs_s, gs_r, os_s, os_r, ox_s, ox_r, oy_s, oy_r,
    z_s, z_r, a_s, a_r, f_s, f_r,
):
    width = e4.shape[1]
    feats = width * Q
    plane = NX * NY
    dp, lat = lax.axis_index("dp"), lax.axis_index("latent")
    c, zhi = lax.rem(dp, 2), lax.div(dp, 2)
    zlo, inplane = lax.div(lat, plane), lax.rem(lat, plane)
    y, x = lax.div(inplane, NX), lax.rem(inplane, NX)
    z = zhi * 2 + zlo
    o = 1 - c
    own = zlo == c

    def at(xx, yy, zz, cc):
        return (lax.div(zz, 2) * 2 + cc, lax.rem(zz, 2) * plane + yy * NX + xx)

    def yof(d):
        return at(x, lax.rem(y + d, NY), z, c)

    def xof(d):
        return at(lax.rem(x + d, NX), y, z, c)

    def zof(d):
        return at(x, y, lax.rem(z + d, NZ), c)

    sibling = at(x, y, z, o)

    def remote(src, dst, send, recv, dev):
        return pltpu.make_async_remote_copy(
            src_ref=src, dst_ref=dst, send_sem=send, recv_sem=recv, device_id=dev, device_id_type=MESH
        )

    def block(cc, xx):
        return pl.ds((cc * NX + xx) * NY, NY)

    xorder = [d for d in (1, 3, 2) if d < NX]
    pending = []

    def go(copy):
        copy.start()
        pending.append(copy)
        return copy

    barrier = pltpu.get_barrier_semaphore()
    partners = [yof(d) for d in range(1, NY)] + [xof(d) for d in range(1, NX)] + [zof(d) for d in range(1, NZ)] + [sibling]
    for dev in partners:
        pl.semaphore_signal(barrier, inc=1, device_id=dev, device_id_type=MESH)
    pl.semaphore_wait(barrier, len(partners))

    def gather_y(buf, k):
        me = buf.at[pl.ds((c * NX + x) * NY + y, 1)]
        return [go(remote(me, me, gy_s.at[k, d - 1], gy_r.at[k, d - 1], yof(d))) for d in range(1, NY)]

    def gather_x(buf, k, ycopies):
        for copy in ycopies:
            copy.wait_recv()
        mine = buf.at[block(c, x)]
        xcopies = {d: go(remote(mine, mine, gx_s.at[k, d - 1], gx_r.at[k, d - 1], xof(d))) for d in xorder}
        forward = {0: go(remote(mine, mine, gs_s.at[k, 0], gs_r.at[k, 0], sibling))}
        return xcopies, forward

    def gather_next(buf, k, xcopies, forward, d):
        xcopies[d].wait_recv()
        got = buf.at[block(c, lax.rem(x + NX - d, NX))]
        forward[d] = go(remote(got, got, gs_s.at[k, d], gs_r.at[k, d], sibling))

    rbuf[pl.ds((c * NX + x) * NY + y, 1)] = to_slab(res_ref, width).astype(BF16)[None]
    ycopies = gather_y(rbuf, 0)

    mask = mask_ref[...].astype(F32)
    upper = (iota((128, 128), 0) <= iota((128, 128), 1)).astype(BF16)
    rank = dot_nn(jnp.broadcast_to(mask, (16, 128)).astype(BF16), upper)[0:1]
    slot = iota((DEAD, 128), 0).astype(F32) + 1.0
    pick = jnp.where((slot == rank) & (mask > 0.5), 1.0, 0.0).astype(BF16)
    pick_ref[...] = pick

    weights = [
        remote(ref, ref, w_s.at[i], w_r.at[i], at(x, y, z + 1 - 2 * zlo, c)) for i, ref in enumerate((e4, w4))
    ]

    @pl.when(own)
    def _():
        for q in range(Q):
            e4[pl.ds(q * DEAD, DEAD), :] = dot_nt(pick, enc_ref[q * width : (q + 1) * width, :]).astype(BF16)
        weights[0].start()
        for q in range(Q):
            w4[pl.ds(q * DEAD, DEAD), :] = dot_nn(pick, dec_ref[:, q * width : (q + 1) * width]).astype(BF16)
        weights[1].start()

    xcopies, forward = gather_x(rbuf, 0, ycopies)

    @pl.when(jnp.logical_not(own))
    def _():
        weights[0].wait_recv()
        weights[1].wait_recv()

    def run_block(cc, xx):
        rows = (NY * SLAB, width)
        here = pl.ds((cc * NX + xx) * NY * SLAB, NY * SLAB)
        pre = fold(dot_nt(rbuf[block(cc, xx)].reshape(rows), e4[...]))
        val = jnp.exp(pre)
        ghost[here, :] = val
        spread = unfold(val)
        aexp[here, :] = spread
        obuf[block(cc, xx)] = dot_nn(spread, w4[...]).astype(BF16).reshape(NY, SLAB, width)

    ocopies, oxcopies = {}, {}

    def add_sibling(d):
        xx = lax.rem(x + NX - d, NX)
        ocopies[d].wait_recv()
        s1[pl.ds(xx * NY, NY)] = (obuf[block(c, xx)].astype(F32) + osib[pl.ds(xx * NY, NY)].astype(F32)).astype(BF16)
        if d:
            t = NX - d
            oxcopies[t] = go(
                remote(s1.at[pl.ds(xx * NY, NY)], xrecv.at[pl.ds((t - 1) * NY, NY)], ox_s.at[t - 1], ox_r.at[t - 1], xof(t))
            )

    order = [0] + xorder
    for i, d in enumerate(order):
        xx = lax.rem(x + NX - d, NX)
        if d:
            gather_next(rbuf, 0, xcopies, forward, d)
        run_block(c, xx)
        forward[d].wait_recv()
        run_block(o, xx)
        ocopies[d] = go(remote(obuf.at[block(o, xx)], osib.at[pl.ds(xx * NY, NY)], os_s.at[d], os_r.at[d], sibling))
        if i > 1:
            add_sibling(order[i - 1])
    add_sibling(order[-1])
    add_sibling(0)

    for d in xorder:
        oxcopies[d].wait_recv()
    oycopies = []
    for d in list(range(1, NY)) + [0]:
        yy = lax.rem(y + d, NY)
        total = s1[pl.ds(x * NY + yy, 1)].astype(F32)
        for t in range(NX - 1):
            total += xrecv[pl.ds(t * NY + yy, 1)].astype(F32)
        if d:
            s2[pl.ds(d - 1, 1)] = total.astype(BF16)
            oycopies.append(
                go(remote(s2.at[pl.ds(d - 1, 1)], yrecv.at[pl.ds(d - 1, 1)], oy_s.at[d - 1], oy_r.at[d - 1], yof(d)))
            )
    out = total[0]
    for d in range(1, NY):
        oycopies[d - 1].wait_recv()
        out += yrecv[d - 1].astype(F32)

    def rms(v):
        squares = jnp.broadcast_to(jnp.sum(v * v, axis=1, keepdims=True), (SLAB, 128))
        return jnp.sqrt(sum_quads(squares) / feats + EPS)[:, 0:1]

    err = to_slab(err_ref, width)
    err_rms = rms(err)
    scale = err_rms / (2.0 * rms(out))
    gbuf[pl.ds((c * NX + x) * NY + y, 1)] = (scale * (scale * out - err) / err_rms).astype(BF16)[None]
    ycopies = gather_y(gbuf, 1)
    xcopies, forward = gather_x(gbuf, 1, ycopies)
    for d in xorder:
        gather_next(gbuf, 1, xcopies, forward, d)
    for d in order:
        forward[d].wait_recv()

    slots = 2 * Q // NZ
    tokens = 2 * plane * SLAB
    tile = min(width, 384)
    factor = 1.0 / math.sqrt(NZ * 2 * plane * 3)

    def gradient(lhs, rhs, base):
        left = lhs[...]
        for j in range(width // tile):
            cols = pl.ds(j * tile, tile)
            part = (dot_tn(left, rhs[:, :, cols].reshape(tokens, tile)) * factor).astype(BF16)
            for q in range(Q):
                zsend[base + q, :, cols] = part[q * DEAD : (q + 1) * DEAD]

    def send_z(first, last):
        for to in range(first // slots, last // slots):

            @pl.when(z != to)
            def _(to=to):
                remote(
                    zsend.at[pl.ds(to * slots, slots)], zrecv.at[z], z_s.at[to], z_r.at[z], at(x, y, to, c)
                ).start()

    gradient(aexp, gbuf, 0)
    send_z(0, Q)
    for b in range(2 * NX):
        here = pl.ds(b * NY * SLAB, NY * SLAB)
        back = fold(dot_nt(gbuf[pl.ds(b * NY, NY)].reshape(NY * SLAB, width), w4[...]))
        pexp[here, :] = unfold(back * ghost[here, :])
    gradient(pexp, rbuf, Q)
    send_z(Q, 2 * Q)

    zrecv[z] = zsend[pl.ds(z * slots, slots)]
    for to in range(NZ):

        @pl.when(z != to)
        def _(to=to):
            remote(
                zsend.at[pl.ds(to * slots, slots)], zrecv.at[to], z_s.at[to], z_r.at[to], at(x, y, to, c)
            ).wait()

    total = zrecv[0].astype(F32)
    for i in range(1, NZ):
        total += zrecv[i].astype(F32)
    zsum[...] = total.astype(BF16)

    def piece(i):
        return zall.at[pl.ds(i * slots, slots)]

    for j in range(NZ // 2):
        to = 2 * j + c

        @pl.when(z != to)
        def _(j=j, to=to):
            remote(zsum, piece(z), a_s.at[j], a_r.at[z], at(x, y, to, c)).start()

    def hand(d):
        i = lax.rem(z + d, NZ)
        return remote(piece(i), piece(i), f_s.at[d], f_r.at[d], sibling)

    @pl.when(own)
    def _():
        zall[pl.ds(z * slots, slots)] = zsum[...]
        for d in range(NZ):
            if d:
                i = lax.rem(z + d, NZ)
                remote(piece(i), piece(i), a_s.at[0], a_r.at[i], sibling).wait_recv()
            hand(d).start()

    @pl.when(jnp.logical_not(own))
    def _():
        for d in range(NZ):
            hand(d).wait_recv()

    for q in range(Q):
        dgrad_ref[:, q * width : (q + 1) * width] = zall[q]
        egrad_ref[:, q * width : (q + 1) * width] = zall[Q + q]

    for j in range(NZ // 2):

        @pl.when(z != 2 * j + c)
        def _(j=j):
            remote(zsum, piece(z), a_s.at[j], a_r.at[0], sibling).wait_send()

    @pl.when(own)
    def _():
        for copy in weights:
            copy.wait_send()
        for d in range(NZ):
            hand(d).wait_send()

    for copy in pending:
        copy.wait_send()


def body(residual, errors, enc_weight, dec_weight, dead_mask):
    feats = residual.shape[1]
    width = feats // Q
    slabs = 2 * NX * NY
    dma = pltpu.SemaphoreType.DMA
    vmem = pl.BlockSpec(memory_space=pltpu.VMEM)
    slots = 2 * Q // NZ
    lines = NX * NY

    def held(n):
        return pltpu.VMEM((n, SLAB, width), BF16)

    dgrad, egrad, pick = pl.pallas_call(
        kernel,
        out_shape=(
            jax.ShapeDtypeStruct((DEAD, feats), BF16),
            jax.ShapeDtypeStruct((DEAD, feats), BF16),
            jax.ShapeDtypeStruct((DEAD, 128), BF16),
        ),
        in_specs=[vmem] * 5,
        out_specs=(vmem,) * 3,
        scratch_shapes=[
            pltpu.VMEM((Q * DEAD, width), BF16),
            pltpu.VMEM((Q * DEAD, width), BF16),
            held(slabs),
            held(slabs),
            held(slabs),
            held(lines),
            held(lines),
            held(lines - NY),
            held(NY - 1),
            held(NY - 1),
            pltpu.VMEM((slabs * SLAB, 2 * DEAD), F32),
            pltpu.VMEM((slabs * SLAB, Q * DEAD), BF16),
            pltpu.VMEM((slabs * SLAB, Q * DEAD), BF16),
            pltpu.VMEM((2 * Q, DEAD, width), BF16),
            pltpu.VMEM((NZ, slots, DEAD, width), BF16),
            pltpu.VMEM((slots, DEAD, width), BF16),
            pltpu.VMEM((2 * Q, DEAD, width), BF16),
            dma((2,)), dma((2,)),
            dma((2, NY - 1)), dma((2, NY - 1)),
            dma((2, NX - 1)), dma((2, NX - 1)),
            dma((2, NX)), dma((2, NX)),
            dma((NX,)), dma((NX,)),
            dma((NX - 1,)), dma((NX - 1,)),
            dma((NY - 1,)), dma((NY - 1,)),
            dma((NZ,)), dma((NZ,)),
            dma((NZ // 2,)), dma((NZ,)),
            dma((NZ,)), dma((NZ,)),
        ],
        compiler_params=pltpu.CompilerParams(
            collective_id=0, has_side_effects=True, vmem_limit_bytes=48 * 1024 * 1024
        ),
    )(residual, errors, enc_weight, dec_weight, dead_mask.reshape(1, -1))
    enc_grad = dot_tn(egrad, pick).astype(BF16)
    dec_grad = dot_tn(pick, dgrad).astype(BF16)
    return enc_grad, dec_grad


def solution(mesh):
    return jax.shard_map(
        body,
        mesh=mesh,
        in_specs=(
            P(("dp", "latent"), None),
            P(("dp", "latent"), None),
            P(None, "latent"),
            P("latent", None),
            P("latent"),
        ),
        out_specs=(P(None, "latent"), P("latent", None)),
        check_vma=False,
    )
```

```python
import math

import jax
import jax.numpy as jnp
from jax import lax
from jax.experimental import pallas as pl
from jax.experimental.pallas import tpu as pltpu
from jax.sharding import PartitionSpec as P

NX, NY, NZ = 4, 8, 8
DEAD = 64
Q = 4
SLAB = 16
EPS = 1e-06
MESH = pl.DeviceIdType.MESH
F32, BF16 = jnp.float32, jnp.bfloat16


def dot_nt(a, b):
    return lax.dot_general(a, b, (((1,), (1,)), ((), ())), preferred_element_type=F32)


def dot_nn(a, b):
    return lax.dot_general(a, b, (((1,), (0,)), ((), ())), preferred_element_type=F32)


def dot_tn(a, b):
    return lax.dot_general(a, b, (((0,), (0,)), ((), ())), preferred_element_type=F32)


def iota(shape, dim):
    return lax.broadcasted_iota(jnp.int32, shape, dim)


def sum_quads(v):
    n = v.shape[0]
    row = iota(v.shape, 0)
    v = v + jnp.where(row % 2 == 0, pltpu.roll(v, n - 1, 0), pltpu.roll(v, 1, 0))
    return v + jnp.where(row % 4 < 2, pltpu.roll(v, n - 2, 0), pltpu.roll(v, 2, 0))


def fold(prod):
    same = iota(prod.shape, 0) % Q == iota(prod.shape, 1) // DEAD
    prod = jnp.where(same, prod, 0.0)
    half = 2 * DEAD
    pair = prod[:, :half] + prod[:, half:]
    return sum_quads(pair + pltpu.roll(pair, DEAD, 1))


def unfold(vals):
    wide = jnp.concatenate([vals, vals], axis=1)
    row = iota(wide.shape, 0)
    keep = (row % Q == iota(wide.shape, 1) // DEAD) & (row % SLAB < 3 * Q)
    return jnp.where(keep, wide, 0.0).astype(BF16)


def to_slab(ref, width):
    rows = iota((SLAB, width), 0)
    out = jnp.zeros((SLAB, width), F32)
    for r in range(3):
        for q in range(Q):
            piece = ref[r : r + 1, q * width : (q + 1) * width].astype(F32)
            out = jnp.where(rows == Q * r + q, piece, out)
    return out


def kernel(
    res_in, err_in, enc_in, dec_in, mask_in,
    dgrad_ref, egrad_ref, pick_ref,
    e4, w4, rbuf, gbuf, obuf, osib, s1, xrecv, s2, yrecv, ghost, aexp, pexp, zsend, zhalf, zrecv, zall,
    res_ref, err_ref, enc_ref, dec_ref, mask_ref, l_s,
    w_s, w_r, gy_s, gy_r, gx_s, gx_r, gs_s, gs_r, os_s, os_r, ox_s, ox_r, oy_s, oy_r,
    h_s, h_r, z_s, z_r, a_s, a_r, f_s, f_r,
):
    width = e4.shape[1]
    loads = [
        pltpu.make_async_copy(src, dst, l_s.at[i])
        for i, (src, dst) in enumerate(
            ((res_in, res_ref), (mask_in, mask_ref), (enc_in, enc_ref), (dec_in, dec_ref), (err_in, err_ref))
        )
    ]
    for load in loads:
        load.start()
    feats = width * Q
    plane = NX * NY
    dp, lat = lax.axis_index("dp"), lax.axis_index("latent")
    c, zhi = lax.rem(dp, 2), lax.div(dp, 2)
    zlo, inplane = lax.div(lat, plane), lax.rem(lat, plane)
    y, x = lax.div(inplane, NX), lax.rem(inplane, NX)
    z = zhi * 2 + zlo
    o = 1 - c
    own = zlo == c

    def at(xx, yy, zz, cc):
        return (lax.div(zz, 2) * 2 + cc, lax.rem(zz, 2) * plane + yy * NX + xx)

    def yof(d):
        return at(x, lax.rem(y + d, NY), z, c)

    def xof(d):
        return at(lax.rem(x + d, NX), y, z, c)

    def zof(d):
        return at(x, y, lax.rem(z + d, NZ), c)

    sibling = at(x, y, z, o)

    def remote(src, dst, send, recv, dev):
        return pltpu.make_async_remote_copy(
            src_ref=src, dst_ref=dst, send_sem=send, recv_sem=recv, device_id=dev, device_id_type=MESH
        )

    def block(cc, xx):
        return pl.ds((cc * NX + xx) * NY, NY)

    xorder = [d for d in (1, 3, 2) if d < NX]
    pending = []

    def go(copy):
        copy.start()
        pending.append(copy)
        return copy

    barrier = pltpu.get_barrier_semaphore()
    partners = [yof(d) for d in range(1, NY)] + [xof(d) for d in range(1, NX)] + [zof(d) for d in range(1, NZ)] + [sibling]
    for dev in partners:
        pl.semaphore_signal(barrier, inc=1, device_id=dev, device_id_type=MESH)
    pl.semaphore_wait(barrier, len(partners))

    cut = width // 256 * 128 + (128 if width % 256 else 0) if width > 128 else 128
    chunks = [pl.ds(0, cut)] + ([pl.ds(cut, width - cut)] if width > cut else [])

    def gather_y(buf, k):
        me = (c * NX + x) * NY + y
        copies = []
        for h, cols in enumerate(chunks):
            part = buf.at[pl.ds(me, 1), :, cols]
            copies.append(
                [go(remote(part, part, gy_s.at[k, h, d - 1], gy_r.at[k, h, d - 1], yof(d))) for d in range(1, NY)]
            )
        return copies

    def gather_x(buf, k, ycopies):
        xcopies = []
        for h, cols in enumerate(chunks):
            for copy in ycopies[h]:
                copy.wait_recv()
            mine = buf.at[block(c, x), :, cols]
            xcopies.append(
                {d: go(remote(mine, mine, gx_s.at[k, h, d - 1], gx_r.at[k, h, d - 1], xof(d))) for d in xorder}
            )
        mine = buf.at[block(c, x)]
        forward = {0: go(remote(mine, mine, gs_s.at[k, 0], gs_r.at[k, 0], sibling))}
        return xcopies, forward

    def gather_next(buf, k, xcopies, forward, d):
        for copies in xcopies:
            copies[d].wait_recv()
        got = buf.at[block(c, lax.rem(x + NX - d, NX))]
        forward[d] = go(remote(got, got, gs_s.at[k, d], gs_r.at[k, d], sibling))

    loads[0].wait()
    rbuf[pl.ds((c * NX + x) * NY + y, 1)] = to_slab(res_ref, width).astype(BF16)[None]
    ycopies = gather_y(rbuf, 0)

    loads[1].wait()
    mask = mask_ref[...].astype(F32)
    upper = (iota((128, 128), 0) <= iota((128, 128), 1)).astype(BF16)
    rank = dot_nn(jnp.broadcast_to(mask, (16, 128)).astype(BF16), upper)[0:1]
    slot = iota((DEAD, 128), 0).astype(F32) + 1.0
    pick = jnp.where((slot == rank) & (mask > 0.5), 1.0, 0.0).astype(BF16)
    pick_ref[...] = pick

    weights = [
        remote(ref, ref, w_s.at[i], w_r.at[i], at(x, y, z + 1 - 2 * zlo, c)) for i, ref in enumerate((e4, w4))
    ]

    loads[2].wait()
    loads[3].wait()
    loads[4].wait()

    @pl.when(own)
    def _():
        for q in range(Q):
            e4[pl.ds(q * DEAD, DEAD), :] = dot_nt(pick, enc_ref[q * width : (q + 1) * width, :]).astype(BF16)
        weights[0].start()
        for q in range(Q):
            w4[pl.ds(q * DEAD, DEAD), :] = dot_nn(pick, dec_ref[:, q * width : (q + 1) * width]).astype(BF16)
        weights[1].start()

    xcopies, forward = gather_x(rbuf, 0, ycopies)

    @pl.when(jnp.logical_not(own))
    def _():
        weights[0].wait_recv()
        weights[1].wait_recv()

    def run_block(cc, xx):
        rows = (NY * SLAB, width)
        here = pl.ds((cc * NX + xx) * NY * SLAB, NY * SLAB)
        pre = fold(dot_nt(rbuf[block(cc, xx)].reshape(rows), e4[...]))
        val = jnp.exp(pre)
        ghost[here, :] = val
        spread = unfold(val)
        aexp[here, :] = spread
        obuf[block(cc, xx)] = dot_nn(spread, w4[...]).astype(BF16).reshape(NY, SLAB, width)

    ocopies, oxcopies = {}, {}

    def add_sibling(d):
        xx = lax.rem(x + NX - d, NX)
        ocopies[d].wait_recv()
        s1[pl.ds(xx * NY, NY)] = (obuf[block(c, xx)].astype(F32) + osib[pl.ds(xx * NY, NY)].astype(F32)).astype(BF16)
        if d:
            t = NX - d
            oxcopies[t] = go(
                remote(s1.at[pl.ds(xx * NY, NY)], xrecv.at[pl.ds((t - 1) * NY, NY)], ox_s.at[t - 1], ox_r.at[t - 1], xof(t))
            )

    order = [0] + xorder
    for i, d in enumerate(order):
        xx = lax.rem(x + NX - d, NX)
        if d:
            gather_next(rbuf, 0, xcopies, forward, d)
        run_block(c, xx)
        forward[d].wait_recv()
        run_block(o, xx)
        ocopies[d] = go(remote(obuf.at[block(o, xx)], osib.at[pl.ds(xx * NY, NY)], os_s.at[d], os_r.at[d], sibling))
        if i > 1:
            add_sibling(order[i - 1])
    add_sibling(order[-1])
    add_sibling(0)

    for d in xorder:
        oxcopies[d].wait_recv()
    oycopies = []
    for d in list(range(1, NY)) + [0]:
        yy = lax.rem(y + d, NY)
        total = s1[pl.ds(x * NY + yy, 1)].astype(F32)
        for t in range(NX - 1):
            total += xrecv[pl.ds(t * NY + yy, 1)].astype(F32)
        if d:
            s2[pl.ds(d - 1, 1)] = total.astype(BF16)
            oycopies.append(
                go(remote(s2.at[pl.ds(d - 1, 1)], yrecv.at[pl.ds(d - 1, 1)], oy_s.at[d - 1], oy_r.at[d - 1], yof(d)))
            )
    out = total[0]
    for d in range(1, NY):
        oycopies[d - 1].wait_recv()
        out += yrecv[d - 1].astype(F32)

    def rms(v):
        squares = jnp.broadcast_to(jnp.sum(v * v, axis=1, keepdims=True), (SLAB, 128))
        return jnp.sqrt(sum_quads(squares) / feats + EPS)[:, 0:1]

    err = to_slab(err_ref, width)
    err_rms = rms(err)
    scale = err_rms / (2.0 * rms(out))
    gbuf[pl.ds((c * NX + x) * NY + y, 1)] = (scale * (scale * out - err) / err_rms).astype(BF16)[None]
    ycopies = gather_y(gbuf, 1)
    xcopies, forward = gather_x(gbuf, 1, ycopies)
    for d in xorder:
        gather_next(gbuf, 1, xcopies, forward, d)
    for d in order:
        forward[d].wait_recv()

    tokens = 2 * plane * SLAB
    tile = min(width, 384)
    factor = 1.0 / math.sqrt(NZ * 2 * plane * 3)
    owners = NZ // 2
    slots = Q // owners
    member = zhi
    half = Q // 2

    def gradient(lhs, rhs, kind):
        left = lhs[...]
        for j in range(width // tile):
            cols = pl.ds(j * tile, tile)
            part = (dot_tn(left, rhs[:, :, cols].reshape(tokens, tile)) * factor).astype(BF16)
            for q in range(Q):
                zsend[kind * Q + q, :, cols] = part[q * DEAD : (q + 1) * DEAD]

    def halves(kind):
        return [
            remote(
                zsend.at[pl.ds(kind * Q + i * half, half)], zhalf.at[pl.ds(kind * Q + i * half, half)],
                h_s.at[kind, i], h_r.at[kind, i], zof(d),
            )
            for i, d in enumerate((1, NZ - 1))
        ]

    def send_halves(kind):
        @pl.when(jnp.logical_not(own))
        def _():
            for copy in halves(kind):
                copy.start()

    def to_member(kind, d):
        m = lax.rem(member + d, owners)
        return remote(
            zsend.at[pl.ds(kind * Q + m * slots, slots)], zrecv.at[kind, d - 1],
            z_s.at[kind, d - 1], z_r.at[kind, d - 1], zof(2 * d),
        )

    def spread_out(kind, d):
        mine = zall.at[pl.ds(kind * Q + member * slots, slots)]
        return remote(mine, mine, a_s.at[kind, d - 1], a_r.at[kind, d - 1], zof(2 * d))

    def hand(kind, d):
        piece = zall.at[pl.ds(kind * Q + lax.rem(member + owners - d, owners) * slots, slots)]
        return remote(piece, piece, f_s.at[kind, d], f_r.at[kind, d], sibling)

    others = [d for d in (1, 3, 2) if d < owners]

    def add_halves(kind):
        for copy in halves(kind):
            copy.wait_recv()
        for i in range(Q):
            p = kind * Q + i
            zsend[p] = (zsend[p].astype(F32) + zhalf[p].astype(F32)).astype(BF16)
        for d in others:
            to_member(kind, d).start()

    def add_members(kind):
        total = zsend[pl.ds(kind * Q + member * slots, slots)].astype(F32)
        for d in others:
            to_member(kind, d).wait_recv()
            total += zrecv[kind, d - 1].astype(F32)
        zall[pl.ds(kind * Q + member * slots, slots)] = total.astype(BF16)
        for d in others:
            spread_out(kind, d).start()
        hand(kind, 0).start()

    def hand_all(kind):
        for d in others:
            spread_out(kind, d).wait_recv()
            hand(kind, d).start()

    gradient(aexp, gbuf, 0)
    send_halves(0)
    for b in range(2 * NX):
        here = pl.ds(b * NY * SLAB, NY * SLAB)
        back = fold(dot_nt(gbuf[pl.ds(b * NY, NY)].reshape(NY * SLAB, width), w4[...]))
        pexp[here, :] = unfold(back * ghost[here, :])

    @pl.when(own)
    def _():
        add_halves(0)

    gradient(pexp, rbuf, 1)
    send_halves(1)

    @pl.when(own)
    def _():
        add_members(0)
        add_halves(1)
        hand_all(0)
        add_members(1)
        hand_all(1)

    @pl.when(jnp.logical_not(own))
    def _():
        for kind in range(2):
            for d in [0] + others:
                hand(kind, d).wait_recv()

    for q in range(Q):
        dgrad_ref[:, q * width : (q + 1) * width] = zall[q]
        egrad_ref[:, q * width : (q + 1) * width] = zall[Q + q]

    @pl.when(own)
    def _():
        for copy in weights:
            copy.wait_send()
        for kind in range(2):
            hand(kind, 0).wait_send()
            for d in others:
                to_member(kind, d).wait_send()
                spread_out(kind, d).wait_send()
                hand(kind, d).wait_send()

    @pl.when(jnp.logical_not(own))
    def _():
        for kind in range(2):
            for copy in halves(kind):
                copy.wait_send()

    for copy in pending:
        copy.wait_send()


def body(residual, errors, enc_weight, dec_weight, dead_mask):
    feats = residual.shape[1]
    width = feats // Q
    slabs = 2 * NX * NY
    dma = pltpu.SemaphoreType.DMA
    vmem = pl.BlockSpec(memory_space=pltpu.VMEM)
    owners = NZ // 2
    lines = NX * NY

    def held(n):
        return pltpu.VMEM((n, SLAB, width), BF16)

    dgrad, egrad, pick = pl.pallas_call(
        kernel,
        out_shape=(
            jax.ShapeDtypeStruct((DEAD, feats), BF16),
            jax.ShapeDtypeStruct((DEAD, feats), BF16),
            jax.ShapeDtypeStruct((DEAD, 128), BF16),
        ),
        in_specs=[pl.BlockSpec(memory_space=pl.ANY)] * 5,
        out_specs=(vmem,) * 3,
        scratch_shapes=[
            pltpu.VMEM((Q * DEAD, width), BF16),
            pltpu.VMEM((Q * DEAD, width), BF16),
            held(slabs),
            held(slabs),
            held(slabs),
            held(lines),
            held(lines),
            held(lines - NY),
            held(NY - 1),
            held(NY - 1),
            pltpu.VMEM((slabs * SLAB, 2 * DEAD), F32),
            pltpu.VMEM((slabs * SLAB, Q * DEAD), BF16),
            pltpu.VMEM((slabs * SLAB, Q * DEAD), BF16),
            pltpu.VMEM((2 * Q, DEAD, width), BF16),
            pltpu.VMEM((2 * Q, DEAD, width), BF16),
            pltpu.VMEM((2, max(owners - 1, 1), Q // owners, DEAD, width), BF16),
            pltpu.VMEM((2 * Q, DEAD, width), BF16),
            pltpu.VMEM(residual.shape, BF16),
            pltpu.VMEM(errors.shape, BF16),
            pltpu.VMEM(enc_weight.shape, BF16),
            pltpu.VMEM(dec_weight.shape, BF16),
            pltpu.VMEM((1, dead_mask.shape[0]), jnp.int32),
            dma((5,)),
            dma((2,)), dma((2,)),
            dma((2, 2, NY - 1)), dma((2, 2, NY - 1)),
            dma((2, 2, NX - 1)), dma((2, 2, NX - 1)),
            dma((2, NX)), dma((2, NX)),
            dma((NX,)), dma((NX,)),
            dma((NX - 1,)), dma((NX - 1,)),
            dma((NY - 1,)), dma((NY - 1,)),
            dma((2, 2)), dma((2, 2)),
            dma((2, max(owners - 1, 1))), dma((2, max(owners - 1, 1))),
            dma((2, max(owners - 1, 1))), dma((2, max(owners - 1, 1))),
            dma((2, owners)), dma((2, owners)),
        ],
        compiler_params=pltpu.CompilerParams(
            collective_id=0, has_side_effects=True, vmem_limit_bytes=56 * 1024 * 1024
        ),
    )(residual, errors, enc_weight, dec_weight, dead_mask.reshape(1, -1))
    enc_grad = dot_tn(egrad, pick).astype(BF16)
    dec_grad = dot_tn(pick, dgrad).astype(BF16)
    return enc_grad, dec_grad


def solution(mesh):
    return jax.shard_map(
        body,
        mesh=mesh,
        in_specs=(
            P(("dp", "latent"), None),
            P(("dp", "latent"), None),
            P(None, "latent"),
            P("latent", None),
            P("latent"),
        ),
        out_specs=(P(None, "latent"), P("latent", None)),
        check_vma=False,
    )
```

```python
import math

import jax
import jax.numpy as jnp
from jax import lax
from jax.experimental import pallas as pl
from jax.experimental.pallas import tpu as pltpu
from jax.sharding import PartitionSpec as P

NX, NY, NZ = 4, 8, 8
DEAD = 64
Q = 4
SLAB = 16
EPS = 1e-06
MESH = pl.DeviceIdType.MESH
F32, BF16 = jnp.float32, jnp.bfloat16


def dot_nt(a, b):
    return lax.dot_general(a, b, (((1,), (1,)), ((), ())), preferred_element_type=F32)


def dot_nn(a, b):
    return lax.dot_general(a, b, (((1,), (0,)), ((), ())), preferred_element_type=F32)


def dot_tn(a, b):
    return lax.dot_general(a, b, (((0,), (0,)), ((), ())), preferred_element_type=F32)


def iota(shape, dim):
    return lax.broadcasted_iota(jnp.int32, shape, dim)


def sum_quads(v):
    n = v.shape[0]
    row = iota(v.shape, 0)
    v = v + jnp.where(row % 2 == 0, pltpu.roll(v, n - 1, 0), pltpu.roll(v, 1, 0))
    return v + jnp.where(row % 4 < 2, pltpu.roll(v, n - 2, 0), pltpu.roll(v, 2, 0))


def fold(prod):
    same = iota(prod.shape, 0) % Q == iota(prod.shape, 1) // DEAD
    prod = jnp.where(same, prod, 0.0)
    half = 2 * DEAD
    pair = prod[:, :half] + prod[:, half:]
    return sum_quads(pair + pltpu.roll(pair, DEAD, 1))


def unfold(vals):
    wide = jnp.concatenate([vals, vals], axis=1)
    row = iota(wide.shape, 0)
    keep = (row % Q == iota(wide.shape, 1) // DEAD) & (row % SLAB < 3 * Q)
    return jnp.where(keep, wide, 0.0).astype(BF16)


def to_slab(ref, width):
    rows = iota((SLAB, width), 0)
    out = jnp.zeros((SLAB, width), F32)
    for r in range(3):
        for q in range(Q):
            piece = ref[r : r + 1, q * width : (q + 1) * width].astype(F32)
            out = jnp.where(rows == Q * r + q, piece, out)
    return out


def kernel(
    res_in, err_in, enc_in, dec_in, mask_in,
    dgrad_ref, egrad_ref, pick_ref,
    e4, w4, rbuf, gbuf, obuf, osib, s1, xrecv, s2, yrecv, ghost, aexp, pexp, zsend, zhalf, zrel, zrecv, zall,
    res_ref, err_ref, enc_ref, dec_ref, mask_ref, l_s,
    w_s, w_r, gy_s, gy_r, gx_s, gx_r, gs_s, gs_r, os_s, os_r, ox_s, ox_r, oy_s, oy_r,
    h_s, h_r, z_s, z_r, a_s, a_r, f_s, f_r,
):
    width = e4.shape[1]
    loads = [
        pltpu.make_async_copy(src, dst, l_s.at[i])
        for i, (src, dst) in enumerate(
            ((res_in, res_ref), (mask_in, mask_ref), (enc_in, enc_ref), (dec_in, dec_ref), (err_in, err_ref))
        )
    ]
    for load in loads:
        load.start()
    feats = width * Q
    plane = NX * NY
    dp, lat = lax.axis_index("dp"), lax.axis_index("latent")
    c, zhi = lax.rem(dp, 2), lax.div(dp, 2)
    zlo, inplane = lax.div(lat, plane), lax.rem(lat, plane)
    y, x = lax.div(inplane, NX), lax.rem(inplane, NX)
    z = zhi * 2 + zlo
    o = 1 - c
    own = zlo == c

    def at(xx, yy, zz, cc):
        return (lax.div(zz, 2) * 2 + cc, lax.rem(zz, 2) * plane + yy * NX + xx)

    def yof(d):
        return at(x, lax.rem(y + d, NY), z, c)

    def xof(d):
        return at(lax.rem(x + d, NX), y, z, c)

    def zof(d):
        return at(x, y, lax.rem(z + d, NZ), c)

    sibling = at(x, y, z, o)

    def remote(src, dst, send, recv, dev):
        return pltpu.make_async_remote_copy(
            src_ref=src, dst_ref=dst, send_sem=send, recv_sem=recv, device_id=dev, device_id_type=MESH
        )

    def block(cc, xx):
        return pl.ds((cc * NX + xx) * NY, NY)

    xorder = [d for d in (1, 3, 2) if d < NX]
    pending = []

    def go(copy):
        copy.start()
        pending.append(copy)
        return copy

    barrier = pltpu.get_barrier_semaphore()
    partners = [yof(d) for d in range(1, NY)] + [xof(d) for d in range(1, NX)] + [zof(d) for d in (1, 2, NZ - 2, NZ - 1)] + [sibling]
    for dev in partners:
        pl.semaphore_signal(barrier, inc=1, device_id=dev, device_id_type=MESH)
    pl.semaphore_wait(barrier, len(partners))

    cut = width // 256 * 128 + (128 if width % 256 else 0) if width > 128 else 128
    chunks = [pl.ds(0, cut)] + ([pl.ds(cut, width - cut)] if width > cut else [])

    def gather_y(buf, k):
        me = (c * NX + x) * NY + y
        copies = []
        for h, cols in enumerate(chunks):
            part = buf.at[pl.ds(me, 1), :, cols]
            copies.append(
                [go(remote(part, part, gy_s.at[k, h, d - 1], gy_r.at[k, h, d - 1], yof(d))) for d in range(1, NY)]
            )
        return copies

    def gather_x(buf, k, ycopies):
        xcopies = []
        for h, cols in enumerate(chunks):
            for copy in ycopies[h]:
                copy.wait_recv()
            mine = buf.at[block(c, x), :, cols]
            xcopies.append(
                {d: go(remote(mine, mine, gx_s.at[k, h, d - 1], gx_r.at[k, h, d - 1], xof(d))) for d in xorder}
            )
        mine = buf.at[block(c, x)]
        forward = {0: go(remote(mine, mine, gs_s.at[k, 0], gs_r.at[k, 0], sibling))}
        return xcopies, forward

    def gather_next(buf, k, xcopies, forward, d):
        for copies in xcopies:
            copies[d].wait_recv()
        got = buf.at[block(c, lax.rem(x + NX - d, NX))]
        forward[d] = go(remote(got, got, gs_s.at[k, d], gs_r.at[k, d], sibling))

    loads[0].wait()
    rbuf[pl.ds((c * NX + x) * NY + y, 1)] = to_slab(res_ref, width).astype(BF16)[None]
    ycopies = gather_y(rbuf, 0)

    loads[1].wait()
    mask = mask_ref[...].astype(F32)
    upper = (iota((128, 128), 0) <= iota((128, 128), 1)).astype(BF16)
    rank = dot_nn(jnp.broadcast_to(mask, (16, 128)).astype(BF16), upper)[0:1]
    slot = iota((DEAD, 128), 0).astype(F32) + 1.0
    pick = jnp.where((slot == rank) & (mask > 0.5), 1.0, 0.0).astype(BF16)
    pick_ref[...] = pick

    weights = [
        remote(ref, ref, w_s.at[i], w_r.at[i], at(x, y, z + 1 - 2 * zlo, c)) for i, ref in enumerate((e4, w4))
    ]

    loads[2].wait()
    loads[3].wait()
    loads[4].wait()

    @pl.when(own)
    def _():
        for q in range(Q):
            e4[pl.ds(q * DEAD, DEAD), :] = dot_nt(pick, enc_ref[q * width : (q + 1) * width, :]).astype(BF16)
        weights[0].start()
        for q in range(Q):
            w4[pl.ds(q * DEAD, DEAD), :] = dot_nn(pick, dec_ref[:, q * width : (q + 1) * width]).astype(BF16)
        weights[1].start()

    xcopies, forward = gather_x(rbuf, 0, ycopies)

    @pl.when(jnp.logical_not(own))
    def _():
        weights[0].wait_recv()
        weights[1].wait_recv()

    def run_block(cc, xx):
        rows = (NY * SLAB, width)
        here = pl.ds((cc * NX + xx) * NY * SLAB, NY * SLAB)
        pre = fold(dot_nt(rbuf[block(cc, xx)].reshape(rows), e4[...]))
        val = jnp.exp(pre)
        ghost[here, :] = val
        spread = unfold(val)
        aexp[here, :] = spread
        obuf[block(cc, xx)] = dot_nn(spread, w4[...]).astype(BF16).reshape(NY, SLAB, width)

    ocopies, oxcopies = {}, {}

    def add_sibling(d):
        xx = lax.rem(x + NX - d, NX)
        ocopies[d].wait_recv()
        s1[pl.ds(xx * NY, NY)] = (obuf[block(c, xx)].astype(F32) + osib[pl.ds(xx * NY, NY)].astype(F32)).astype(BF16)
        if d:
            t = NX - d
            oxcopies[t] = go(
                remote(s1.at[pl.ds(xx * NY, NY)], xrecv.at[pl.ds((t - 1) * NY, NY)], ox_s.at[t - 1], ox_r.at[t - 1], xof(t))
            )

    order = [0] + xorder
    for i, d in enumerate(order):
        xx = lax.rem(x + NX - d, NX)
        if d:
            gather_next(rbuf, 0, xcopies, forward, d)
        run_block(c, xx)
        forward[d].wait_recv()
        run_block(o, xx)
        ocopies[d] = go(remote(obuf.at[block(o, xx)], osib.at[pl.ds(xx * NY, NY)], os_s.at[d], os_r.at[d], sibling))
        if i > 1:
            add_sibling(order[i - 1])
    add_sibling(order[-1])
    add_sibling(0)

    for d in xorder:
        oxcopies[d].wait_recv()
    oycopies = []
    for d in list(range(1, NY)) + [0]:
        yy = lax.rem(y + d, NY)
        total = s1[pl.ds(x * NY + yy, 1)].astype(F32)
        for t in range(NX - 1):
            total += xrecv[pl.ds(t * NY + yy, 1)].astype(F32)
        if d:
            s2[pl.ds(d - 1, 1)] = total.astype(BF16)
            oycopies.append(
                go(remote(s2.at[pl.ds(d - 1, 1)], yrecv.at[pl.ds(d - 1, 1)], oy_s.at[d - 1], oy_r.at[d - 1], yof(d)))
            )
    out = total[0]
    for d in range(1, NY):
        oycopies[d - 1].wait_recv()
        out += yrecv[d - 1].astype(F32)

    def rms(v):
        squares = jnp.broadcast_to(jnp.sum(v * v, axis=1, keepdims=True), (SLAB, 128))
        return jnp.sqrt(sum_quads(squares) / feats + EPS)[:, 0:1]

    err = to_slab(err_ref, width)
    err_rms = rms(err)
    scale = err_rms / (2.0 * rms(out))
    gbuf[pl.ds((c * NX + x) * NY + y, 1)] = (scale * (scale * out - err) / err_rms).astype(BF16)[None]
    ycopies = gather_y(gbuf, 1)
    xcopies, forward = gather_x(gbuf, 1, ycopies)
    for d in xorder:
        gather_next(gbuf, 1, xcopies, forward, d)
    for d in order:
        forward[d].wait_recv()

    tokens = 2 * plane * SLAB
    tile = min(width, 384)
    factor = 1.0 / math.sqrt(NZ * 2 * plane * 3)
    to_left = lax.rem(zhi + Q - 1, Q)
    to_right = lax.rem(zhi + 1, Q)
    across = lax.rem(zhi + 2, Q)
    right, left = zof(2), zof(NZ - 2)
    top, low = pl.ds(0, DEAD // 2), pl.ds(DEAD // 2, DEAD // 2)
    half = Q // 2

    def gradient(lhs, rhs, kind):
        left = lhs[...]
        for j in range(width // tile):
            cols = pl.ds(j * tile, tile)
            part = (dot_tn(left, rhs[:, :, cols].reshape(tokens, tile)) * factor).astype(BF16)
            for q in range(Q):
                zsend[kind * Q + q, :, cols] = part[q * DEAD : (q + 1) * DEAD]

    def halves(kind):
        return [
            remote(
                zsend.at[pl.ds(kind * Q + i * half, half)], zhalf.at[pl.ds(kind * Q + i * half, half)],
                h_s.at[kind, i], h_r.at[kind, i], zof(d),
            )
            for i, d in enumerate((1, NZ - 1))
        ]

    def send_halves(kind):
        @pl.when(jnp.logical_not(own))
        def _():
            for copy in halves(kind):
                copy.start()

    def z_copy(kind, i):
        k = kind * Q
        pairs = (
            (zsend.at[k + across, top], zrel.at[kind, 0], right),
            (zsend.at[k + across, low], zrel.at[kind, 1], left),
            (zsend.at[k + to_right, low], zrecv.at[kind, 0, low], right),
            (zsend.at[k + to_left, top], zrecv.at[kind, 1, top], left),
            (zsend.at[k + to_right, top], zrecv.at[kind, 0, top], right),
            (zsend.at[k + to_left, low], zrecv.at[kind, 1, low], left),
        )
        src, dst, dev = pairs[i]
        return remote(src, dst, z_s.at[kind, i], z_r.at[kind, i], dev)

    def a_copy(kind, i):
        sent = (
            (zhi, top, right), (zhi, low, left), (zhi, low, right), (zhi, top, left),
            (to_left, top, right), (to_right, low, left),
        )
        p, rows, dev = sent[i]
        part = zall.at[kind * Q + p, rows]
        return remote(part, part, a_s.at[kind, i], a_r.at[kind, i], dev)

    def hand(kind, i):
        piece = zall.at[kind * Q + (zhi, to_left, to_right, across)[i]]
        return remote(piece, piece, f_s.at[kind, i], f_r.at[kind, i], sibling)

    def add_halves(kind):
        for copy in halves(kind):
            copy.wait_recv()
        for p, sends in ((across, (0, 1)), (to_right, (2,)), (to_left, (3,)), (zhi, ())):
            p = kind * Q + p
            zsend[p] = (zsend[p].astype(F32) + zhalf[p].astype(F32)).astype(BF16)
            for i in sends:
                z_copy(kind, i).start()

    def relay(kind):
        for i, p, rows in ((0, to_right, top), (1, to_left, low)):
            z_copy(kind, i).wait_recv()
            p = kind * Q + p
            zsend[p, rows] = (zsend[p, rows].astype(F32) + zrel[kind, i].astype(F32)).astype(BF16)
            z_copy(kind, 4 + i).start()

    def add_members(kind):
        for i in range(2, 6):
            z_copy(kind, i).wait_recv()
        p = kind * Q + zhi
        zall[p] = (zsend[p].astype(F32) + zrecv[kind, 0].astype(F32) + zrecv[kind, 1].astype(F32)).astype(BF16)
        for i in range(4):
            a_copy(kind, i).start()
        hand(kind, 0).start()

    def share(kind):
        for i in range(2):
            a_copy(kind, i).wait_recv()
            a_copy(kind, 4 + i).start()
        for i in range(2):
            a_copy(kind, 2 + i).wait_recv()
            hand(kind, 1 + i).start()

    def finish(kind):
        for i in range(4, 6):
            a_copy(kind, i).wait_recv()
        hand(kind, 3).start()

    gradient(aexp, gbuf, 0)
    send_halves(0)
    for b in range(2 * NX):
        here = pl.ds(b * NY * SLAB, NY * SLAB)
        back = fold(dot_nt(gbuf[pl.ds(b * NY, NY)].reshape(NY * SLAB, width), w4[...]))
        pexp[here, :] = unfold(back * ghost[here, :])

    @pl.when(own)
    def _():
        add_halves(0)

    gradient(pexp, rbuf, 1)
    send_halves(1)

    @pl.when(own)
    def _():
        relay(0)
        add_halves(1)
        add_members(0)
        relay(1)
        share(0)
        add_members(1)
        finish(0)
        share(1)
        finish(1)

    @pl.when(jnp.logical_not(own))
    def _():
        for kind in range(2):
            for i in range(Q):
                hand(kind, i).wait_recv()

    for q in range(Q):
        dgrad_ref[:, q * width : (q + 1) * width] = zall[q]
        egrad_ref[:, q * width : (q + 1) * width] = zall[Q + q]

    @pl.when(own)
    def _():
        for copy in weights:
            copy.wait_send()
        for kind in range(2):
            for i in range(6):
                z_copy(kind, i).wait_send()
                a_copy(kind, i).wait_send()
            for i in range(Q):
                hand(kind, i).wait_send()

    @pl.when(jnp.logical_not(own))
    def _():
        for kind in range(2):
            for copy in halves(kind):
                copy.wait_send()

    for copy in pending:
        copy.wait_send()


def body(residual, errors, enc_weight, dec_weight, dead_mask):
    feats = residual.shape[1]
    width = feats // Q
    slabs = 2 * NX * NY
    dma = pltpu.SemaphoreType.DMA
    vmem = pl.BlockSpec(memory_space=pltpu.VMEM)
    lines = NX * NY

    def held(n):
        return pltpu.VMEM((n, SLAB, width), BF16)

    dgrad, egrad, pick = pl.pallas_call(
        kernel,
        out_shape=(
            jax.ShapeDtypeStruct((DEAD, feats), BF16),
            jax.ShapeDtypeStruct((DEAD, feats), BF16),
            jax.ShapeDtypeStruct((DEAD, 128), BF16),
        ),
        in_specs=[pl.BlockSpec(memory_space=pl.ANY)] * 5,
        out_specs=(vmem,) * 3,
        scratch_shapes=[
            pltpu.VMEM((Q * DEAD, width), BF16),
            pltpu.VMEM((Q * DEAD, width), BF16),
            held(slabs),
            held(slabs),
            held(slabs),
            held(lines),
            held(lines),
            held(lines - NY),
            held(NY - 1),
            held(NY - 1),
            pltpu.VMEM((slabs * SLAB, 2 * DEAD), F32),
            pltpu.VMEM((slabs * SLAB, Q * DEAD), BF16),
            pltpu.VMEM((slabs * SLAB, Q * DEAD), BF16),
            pltpu.VMEM((2 * Q, DEAD, width), BF16),
            pltpu.VMEM((2 * Q, DEAD, width), BF16),
            pltpu.VMEM((2, 2, DEAD // 2, width), BF16),
            pltpu.VMEM((2, 2, DEAD, width), BF16),
            pltpu.VMEM((2 * Q, DEAD, width), BF16),
            pltpu.VMEM(residual.shape, BF16),
            pltpu.VMEM(errors.shape, BF16),
            pltpu.VMEM(enc_weight.shape, BF16),
            pltpu.VMEM(dec_weight.shape, BF16),
            pltpu.VMEM((1, dead_mask.shape[0]), jnp.int32),
            dma((5,)),
            dma((2,)), dma((2,)),
            dma((2, 2, NY - 1)), dma((2, 2, NY - 1)),
            dma((2, 2, NX - 1)), dma((2, 2, NX - 1)),
            dma((2, NX)), dma((2, NX)),
            dma((NX,)), dma((NX,)),
            dma((NX - 1,)), dma((NX - 1,)),
            dma((NY - 1,)), dma((NY - 1,)),
            dma((2, 2)), dma((2, 2)),
            dma((2, 6)), dma((2, 6)),
            dma((2, 6)), dma((2, 6)),
            dma((2, Q)), dma((2, Q)),
        ],
        compiler_params=pltpu.CompilerParams(
            collective_id=0, has_side_effects=True, vmem_limit_bytes=56 * 1024 * 1024
        ),
    )(residual, errors, enc_weight, dec_weight, dead_mask.reshape(1, -1))
    enc_grad = dot_tn(egrad, pick).astype(BF16)
    dec_grad = dot_tn(pick, dgrad).astype(BF16)
    return enc_grad, dec_grad


def solution(mesh):
    return jax.shard_map(
        body,
        mesh=mesh,
        in_specs=(
            P(("dp", "latent"), None),
            P(("dp", "latent"), None),
            P(None, "latent"),
            P("latent", None),
            P("latent"),
        ),
        out_specs=(P(None, "latent"), P("latent", None)),
        check_vma=False,
    )
```

```python
import math

import jax
import jax.numpy as jnp
from jax import lax
from jax.experimental import pallas as pl
from jax.experimental.pallas import tpu as pltpu
from jax.sharding import PartitionSpec as P

NX, NY, NZ = 4, 8, 8
DEAD = 64
Q = 4
SLAB = 16
REAL = 3 * Q
EPS = 1e-06
MESH = pl.DeviceIdType.MESH
F32, BF16 = jnp.float32, jnp.bfloat16


def dot_nt(a, b):
    return lax.dot_general(a, b, (((1,), (1,)), ((), ())), preferred_element_type=F32)


def dot_nn(a, b):
    return lax.dot_general(a, b, (((1,), (0,)), ((), ())), preferred_element_type=F32)


def dot_tn(a, b):
    return lax.dot_general(a, b, (((0,), (0,)), ((), ())), preferred_element_type=F32)


def iota(shape, dim):
    return lax.broadcasted_iota(jnp.int32, shape, dim)


def sum_quads(v):
    n = v.shape[0]
    row = iota(v.shape, 0)
    v = v + jnp.where(row % 2 == 0, pltpu.roll(v, n - 1, 0), pltpu.roll(v, 1, 0))
    return v + jnp.where(row % 4 < 2, pltpu.roll(v, n - 2, 0), pltpu.roll(v, 2, 0))


def fold(prod):
    same = iota(prod.shape, 0) % Q == iota(prod.shape, 1) // DEAD
    prod = jnp.where(same, prod, 0.0)
    half = 2 * DEAD
    pair = prod[:, :half] + prod[:, half:]
    return sum_quads(pair + pltpu.roll(pair, DEAD, 1))


def unfold(vals):
    wide = jnp.concatenate([vals, vals], axis=1)
    row = iota(wide.shape, 0)
    return jnp.where(row % Q == iota(wide.shape, 1) // DEAD, wide, 0.0).astype(BF16)


def to_slab(ref, width):
    rows = iota((SLAB, width), 0)
    out = jnp.zeros((SLAB, width), F32)
    for r in range(3):
        for q in range(Q):
            piece = ref[r : r + 1, q * width : (q + 1) * width].astype(F32)
            out = jnp.where(rows == Q * r + q, piece, out)
    return out


def kernel(
    res_in, err_in, enc_in, dec_in, mask_in,
    dgrad_ref, egrad_ref, pick_ref,
    e4, w4, ybuf, rbuf, gbuf, obuf, osib, s1, xrecv, s2, yrecv, ghost, aexp, pexp, zsend, zhalf, zrel, zrecv, zall,
    res_ref, err_ref, enc_ref, dec_ref, mask_ref, l_s,
    w_s, w_r, gy_s, gy_r, gx_s, gx_r, gs_s, gs_r, os_s, os_r, ox_s, ox_r, oy_s, oy_r,
    h_s, h_r, z_s, z_r, a_s, a_r, f_s, f_r,
):
    width = e4.shape[1]
    loads = [
        pltpu.make_async_copy(src, dst, l_s.at[i])
        for i, (src, dst) in enumerate(
            ((res_in, res_ref), (mask_in, mask_ref), (enc_in, enc_ref), (dec_in, dec_ref), (err_in, err_ref))
        )
    ]
    for load in loads:
        load.start()
    feats = width * Q
    plane = NX * NY
    dp, lat = lax.axis_index("dp"), lax.axis_index("latent")
    c, zhi = lax.rem(dp, 2), lax.div(dp, 2)
    zlo, inplane = lax.div(lat, plane), lax.rem(lat, plane)
    y, x = lax.div(inplane, NX), lax.rem(inplane, NX)
    z = zhi * 2 + zlo
    o = 1 - c
    own = zlo == c

    def at(xx, yy, zz, cc):
        return (lax.div(zz, 2) * 2 + cc, lax.rem(zz, 2) * plane + yy * NX + xx)

    def yof(d):
        return at(x, lax.rem(y + d, NY), z, c)

    def xof(d):
        return at(lax.rem(x + d, NX), y, z, c)

    def zof(d):
        return at(x, y, lax.rem(z + d, NZ), c)

    sibling = at(x, y, z, o)

    def remote(src, dst, send, recv, dev):
        return pltpu.make_async_remote_copy(
            src_ref=src, dst_ref=dst, send_sem=send, recv_sem=recv, device_id=dev, device_id_type=MESH
        )

    def block(cc, xx):
        return pl.ds(cc * NX + xx, 1)

    xorder = [d for d in (1, 3, 2) if d < NX]
    pending = []

    def go(copy):
        copy.start()
        pending.append(copy)
        return copy

    barrier = pltpu.get_barrier_semaphore()
    partners = [yof(d) for d in range(1, NY)] + [xof(d) for d in range(1, NX)] + [zof(d) for d in (1, 2, NZ - 2, NZ - 1)] + [sibling]
    for dev in partners:
        pl.semaphore_signal(barrier, inc=1, device_id=dev, device_id_type=MESH)
    pl.semaphore_wait(barrier, len(partners))

    cut = width // 256 * 128 + (128 if width % 256 else 0) if width > 128 else 128
    chunks = [pl.ds(0, cut)] + ([pl.ds(cut, width - cut)] if width > cut else [])

    line = NY * REAL
    slot, place = iota((line, NY * SLAB), 0), iota((line, NY * SLAB), 1)
    pack = jnp.where(slot // REAL * SLAB + slot % REAL == place, 1.0, 0.0).astype(BF16)

    def gather_y(k):
        copies = []
        for h, cols in enumerate(chunks):
            part = ybuf.at[k, pl.ds(y, 1), :, cols]
            copies.append(
                [go(remote(part, part, gy_s.at[k, h, d - 1], gy_r.at[k, h, d - 1], yof(d))) for d in range(1, NY)]
            )
        return copies

    def gather_x(buf, k, ycopies):
        xcopies = []
        for h, cols in enumerate(chunks):
            for copy in ycopies[h]:
                copy.wait_recv()
            slabs = ybuf[k, :, :, cols].reshape(NY * SLAB, -1)
            buf[block(c, x), :, cols] = dot_nn(pack, slabs).astype(BF16)[None]
            mine = buf.at[block(c, x), :, cols]
            xcopies.append(
                {d: go(remote(mine, mine, gx_s.at[k, h, d - 1], gx_r.at[k, h, d - 1], xof(d))) for d in xorder}
            )
        mine = buf.at[block(c, x)]
        forward = {0: go(remote(mine, mine, gs_s.at[k, 0], gs_r.at[k, 0], sibling))}
        return xcopies, forward

    def gather_next(buf, k, xcopies, forward, d):
        for copies in xcopies:
            copies[d].wait_recv()
        got = buf.at[block(c, lax.rem(x + NX - d, NX))]
        forward[d] = go(remote(got, got, gs_s.at[k, d], gs_r.at[k, d], sibling))

    loads[0].wait()
    ybuf[0, pl.ds(y, 1)] = to_slab(res_ref, width).astype(BF16)[None]
    ycopies = gather_y(0)

    loads[1].wait()
    mask = mask_ref[...].astype(F32)
    upper = (iota((128, 128), 0) <= iota((128, 128), 1)).astype(BF16)
    rank = dot_nn(jnp.broadcast_to(mask, (16, 128)).astype(BF16), upper)[0:1]
    order = iota((DEAD, 128), 0).astype(F32) + 1.0
    pick = jnp.where((order == rank) & (mask > 0.5), 1.0, 0.0).astype(BF16)
    pick_ref[...] = pick

    weights = [
        remote(ref, ref, w_s.at[i], w_r.at[i], at(x, y, z + 1 - 2 * zlo, c)) for i, ref in enumerate((e4, w4))
    ]

    loads[2].wait()
    loads[3].wait()
    loads[4].wait()

    @pl.when(own)
    def _():
        for q in range(Q):
            e4[pl.ds(q * DEAD, DEAD), :] = dot_nt(pick, enc_ref[q * width : (q + 1) * width, :]).astype(BF16)
        weights[0].start()
        for q in range(Q):
            w4[pl.ds(q * DEAD, DEAD), :] = dot_nn(pick, dec_ref[:, q * width : (q + 1) * width]).astype(BF16)
        weights[1].start()

    xcopies, forward = gather_x(rbuf, 0, ycopies)

    @pl.when(jnp.logical_not(own))
    def _():
        weights[0].wait_recv()
        weights[1].wait_recv()

    def run_block(cc, xx):
        b = cc * NX + xx
        here = pl.ds(pl.multiple_of(b * line, 32 if line % 32 == 0 else 8), line)
        pre = fold(dot_nt(rbuf[b], e4[...]))
        val = jnp.exp(pre)
        ghost[here, :] = val
        spread = unfold(val)
        aexp[here, :] = spread
        obuf[b] = dot_nn(spread, w4[...]).astype(BF16)

    ocopies, oxcopies = {}, {}

    def add_sibling(d):
        xx = lax.rem(x + NX - d, NX)
        ocopies[d].wait_recv()
        s1[xx] = (obuf[c * NX + xx].astype(F32) + osib[xx].astype(F32)).astype(BF16)
        if d:
            t = NX - d
            oxcopies[t] = go(
                remote(s1.at[xx], xrecv.at[t - 1], ox_s.at[t - 1], ox_r.at[t - 1], xof(t))
            )

    order = [0] + xorder
    for i, d in enumerate(order):
        xx = lax.rem(x + NX - d, NX)
        if d:
            gather_next(rbuf, 0, xcopies, forward, d)
        run_block(c, xx)
        forward[d].wait_recv()
        run_block(o, xx)
        ocopies[d] = go(remote(obuf.at[o * NX + xx], osib.at[xx], os_s.at[d], os_r.at[d], sibling))
        if i > 1:
            add_sibling(order[i - 1])
    add_sibling(order[-1])
    add_sibling(0)

    for d in xorder:
        oxcopies[d].wait_recv()
    total = s1[x].astype(F32)
    for t in range(NX - 1):
        total += xrecv[t].astype(F32)
    s2[...] = dot_tn(pack, total.astype(BF16)).astype(BF16).reshape(NY, SLAB, width)
    oycopies = []
    for d in range(1, NY):
        oycopies.append(
            go(remote(s2.at[lax.rem(y + d, NY)], yrecv.at[d - 1], oy_s.at[d - 1], oy_r.at[d - 1], yof(d)))
        )
    out = s2[y].astype(F32)
    for d in range(1, NY):
        oycopies[d - 1].wait_recv()
        out += yrecv[d - 1].astype(F32)

    def rms(v):
        squares = jnp.broadcast_to(jnp.sum(v * v, axis=1, keepdims=True), (SLAB, 128))
        return jnp.sqrt(sum_quads(squares) / feats + EPS)[:, 0:1]

    err = to_slab(err_ref, width)
    err_rms = rms(err)
    scale = err_rms / (2.0 * rms(out))
    ybuf[1, pl.ds(y, 1)] = (scale * (scale * out - err) / err_rms).astype(BF16)[None]
    ycopies = gather_y(1)
    xcopies, forward = gather_x(gbuf, 1, ycopies)
    for d in xorder:
        gather_next(gbuf, 1, xcopies, forward, d)
    for d in order:
        forward[d].wait_recv()

    tokens = 2 * plane * REAL
    tile = min(width, 384)
    factor = 1.0 / math.sqrt(NZ * 2 * plane * 3)
    to_left = lax.rem(zhi + Q - 1, Q)
    to_right = lax.rem(zhi + 1, Q)
    across = lax.rem(zhi + 2, Q)
    right, left = zof(2), zof(NZ - 2)
    top, low = pl.ds(0, DEAD // 2), pl.ds(DEAD // 2, DEAD // 2)
    half = Q // 2

    def gradient(lhs, rhs, kind):
        left = lhs[...]
        for j in range(width // tile):
            cols = pl.ds(j * tile, tile)
            part = (dot_tn(left, rhs[:, :, cols].reshape(tokens, tile)) * factor).astype(BF16)
            for q in range(Q):
                zsend[kind * Q + q, :, cols] = part[q * DEAD : (q + 1) * DEAD]

    def halves(kind):
        return [
            remote(
                zsend.at[pl.ds(kind * Q + i * half, half)], zhalf.at[pl.ds(kind * Q + i * half, half)],
                h_s.at[kind, i], h_r.at[kind, i], zof(d),
            )
            for i, d in enumerate((1, NZ - 1))
        ]

    def send_halves(kind):
        @pl.when(jnp.logical_not(own))
        def _():
            for copy in halves(kind):
                copy.start()

    def z_copy(kind, i):
        k = kind * Q
        pairs = (
            (zsend.at[k + across, top], zrel.at[kind, 0], right),
            (zsend.at[k + across, low], zrel.at[kind, 1], left),
            (zsend.at[k + to_right, low], zrecv.at[kind, 0, low], right),
            (zsend.at[k + to_left, top], zrecv.at[kind, 1, top], left),
            (zsend.at[k + to_right, top], zrecv.at[kind, 0, top], right),
            (zsend.at[k + to_left, low], zrecv.at[kind, 1, low], left),
        )
        src, dst, dev = pairs[i]
        return remote(src, dst, z_s.at[kind, i], z_r.at[kind, i], dev)

    def a_copy(kind, i):
        sent = (
            (zhi, top, right), (zhi, low, left), (zhi, low, right), (zhi, top, left),
            (to_left, top, right), (to_right, low, left),
        )
        p, rows, dev = sent[i]
        part = zall.at[kind * Q + p, rows]
        return remote(part, part, a_s.at[kind, i], a_r.at[kind, i], dev)

    def hand(kind, i):
        piece = zall.at[kind * Q + (zhi, to_left, to_right, across)[i]]
        return remote(piece, piece, f_s.at[kind, i], f_r.at[kind, i], sibling)

    def add_halves(kind):
        for copy in halves(kind):
            copy.wait_recv()
        for p, sends in ((across, (0, 1)), (to_right, (2,)), (to_left, (3,)), (zhi, ())):
            p = kind * Q + p
            zsend[p] = (zsend[p].astype(F32) + zhalf[p].astype(F32)).astype(BF16)
            for i in sends:
                z_copy(kind, i).start()

    def relay(kind):
        for i, p, rows in ((0, to_right, top), (1, to_left, low)):
            z_copy(kind, i).wait_recv()
            p = kind * Q + p
            zsend[p, rows] = (zsend[p, rows].astype(F32) + zrel[kind, i].astype(F32)).astype(BF16)
            z_copy(kind, 4 + i).start()

    def add_members(kind):
        for i in range(2, 6):
            z_copy(kind, i).wait_recv()
        p = kind * Q + zhi
        zall[p] = (zsend[p].astype(F32) + zrecv[kind, 0].astype(F32) + zrecv[kind, 1].astype(F32)).astype(BF16)
        for i in range(4):
            a_copy(kind, i).start()
        hand(kind, 0).start()

    def share(kind):
        for i in range(2):
            a_copy(kind, i).wait_recv()
            a_copy(kind, 4 + i).start()
        for i in range(2):
            a_copy(kind, 2 + i).wait_recv()
            hand(kind, 1 + i).start()

    def finish(kind):
        for i in range(4, 6):
            a_copy(kind, i).wait_recv()
        hand(kind, 3).start()

    gradient(aexp, gbuf, 0)
    send_halves(0)
    for b in range(2 * NX):
        here = pl.ds(b * line, line)
        back = fold(dot_nt(gbuf[b], w4[...]))
        pexp[here, :] = unfold(back * ghost[here, :])

    @pl.when(own)
    def _():
        add_halves(0)

    gradient(pexp, rbuf, 1)
    send_halves(1)

    @pl.when(own)
    def _():
        relay(0)
        add_halves(1)
        add_members(0)
        relay(1)
        share(0)
        add_members(1)
        finish(0)
        share(1)
        finish(1)

    @pl.when(jnp.logical_not(own))
    def _():
        for kind in range(2):
            for i in range(Q):
                hand(kind, i).wait_recv()

    for q in range(Q):
        dgrad_ref[:, q * width : (q + 1) * width] = zall[q]
        egrad_ref[:, q * width : (q + 1) * width] = zall[Q + q]

    @pl.when(own)
    def _():
        for copy in weights:
            copy.wait_send()
        for kind in range(2):
            for i in range(6):
                z_copy(kind, i).wait_send()
                a_copy(kind, i).wait_send()
            for i in range(Q):
                hand(kind, i).wait_send()

    @pl.when(jnp.logical_not(own))
    def _():
        for kind in range(2):
            for copy in halves(kind):
                copy.wait_send()

    for copy in pending:
        copy.wait_send()


def body(residual, errors, enc_weight, dec_weight, dead_mask):
    feats = residual.shape[1]
    width = feats // Q
    line = NY * REAL
    dma = pltpu.SemaphoreType.DMA
    vmem = pl.BlockSpec(memory_space=pltpu.VMEM)

    def held(n):
        return pltpu.VMEM((n, line, width), BF16)

    dgrad, egrad, pick = pl.pallas_call(
        kernel,
        out_shape=(
            jax.ShapeDtypeStruct((DEAD, feats), BF16),
            jax.ShapeDtypeStruct((DEAD, feats), BF16),
            jax.ShapeDtypeStruct((DEAD, 128), BF16),
        ),
        in_specs=[pl.BlockSpec(memory_space=pl.ANY)] * 5,
        out_specs=(vmem,) * 3,
        scratch_shapes=[
            pltpu.VMEM((Q * DEAD, width), BF16),
            pltpu.VMEM((Q * DEAD, width), BF16),
            pltpu.VMEM((2, NY, SLAB, width), BF16),
            held(2 * NX),
            held(2 * NX),
            held(2 * NX),
            held(NX),
            held(NX),
            held(NX - 1),
            pltpu.VMEM((NY, SLAB, width), BF16),
            pltpu.VMEM((NY - 1, SLAB, width), BF16),
            pltpu.VMEM((2 * NX * line, 2 * DEAD), F32),
            pltpu.VMEM((2 * NX * line, Q * DEAD), BF16),
            pltpu.VMEM((2 * NX * line, Q * DEAD), BF16),
            pltpu.VMEM((2 * Q, DEAD, width), BF16),
            pltpu.VMEM((2 * Q, DEAD, width), BF16),
            pltpu.VMEM((2, 2, DEAD // 2, width), BF16),
            pltpu.VMEM((2, 2, DEAD, width), BF16),
            pltpu.VMEM((2 * Q, DEAD, width), BF16),
            pltpu.VMEM(residual.shape, BF16),
            pltpu.VMEM(errors.shape, BF16),
            pltpu.VMEM(enc_weight.shape, BF16),
            pltpu.VMEM(dec_weight.shape, BF16),
            pltpu.VMEM((1, dead_mask.shape[0]), jnp.int32),
            dma((5,)),
            dma((2,)), dma((2,)),
            dma((2, 2, NY - 1)), dma((2, 2, NY - 1)),
            dma((2, 2, NX - 1)), dma((2, 2, NX - 1)),
            dma((2, NX)), dma((2, NX)),
            dma((NX,)), dma((NX,)),
            dma((NX - 1,)), dma((NX - 1,)),
            dma((NY - 1,)), dma((NY - 1,)),
            dma((2, 2)), dma((2, 2)),
            dma((2, 6)), dma((2, 6)),
            dma((2, 6)), dma((2, 6)),
            dma((2, Q)), dma((2, Q)),
        ],
        compiler_params=pltpu.CompilerParams(
            collective_id=0, has_side_effects=True, vmem_limit_bytes=56 * 1024 * 1024
        ),
    )(residual, errors, enc_weight, dec_weight, dead_mask.reshape(1, -1))
    enc_grad = dot_tn(egrad, pick).astype(BF16)
    dec_grad = dot_tn(pick, dgrad).astype(BF16)
    return enc_grad, dec_grad


def solution(mesh):
    return jax.shard_map(
        body,
        mesh=mesh,
        in_specs=(
            P(("dp", "latent"), None),
            P(("dp", "latent"), None),
            P(None, "latent"),
            P("latent", None),
            P("latent"),
        ),
        out_specs=(P(None, "latent"), P("latent", None)),
        check_vma=False,
    )
```

```python
import math

import jax
import jax.numpy as jnp
from jax import lax
from jax.experimental import pallas as pl
from jax.experimental.pallas import tpu as pltpu
from jax.sharding import PartitionSpec as P

NX, NY, NZ = 4, 8, 8
DEAD = 64
Q = 4
SLAB = 16
REAL = 3 * Q
EPS = 1e-06
MESH = pl.DeviceIdType.MESH
F32, BF16 = jnp.float32, jnp.bfloat16


def dot_nt(a, b):
    return lax.dot_general(a, b, (((1,), (1,)), ((), ())), preferred_element_type=F32)


def dot_nn(a, b):
    return lax.dot_general(a, b, (((1,), (0,)), ((), ())), preferred_element_type=F32)


def dot_tn(a, b):
    return lax.dot_general(a, b, (((0,), (0,)), ((), ())), preferred_element_type=F32)


def iota(shape, dim):
    return lax.broadcasted_iota(jnp.int32, shape, dim)


def sum_quads(v):
    n = v.shape[0]
    row = iota(v.shape, 0)
    v = v + jnp.where(row % 2 == 0, pltpu.roll(v, n - 1, 0), pltpu.roll(v, 1, 0))
    return v + jnp.where(row % 4 < 2, pltpu.roll(v, n - 2, 0), pltpu.roll(v, 2, 0))


def fold(prod):
    same = iota(prod.shape, 0) % Q == iota(prod.shape, 1) // DEAD
    prod = jnp.where(same, prod, 0.0)
    half = 2 * DEAD
    pair = prod[:, :half] + prod[:, half:]
    return sum_quads(pair + pltpu.roll(pair, DEAD, 1))


def unfold(vals):
    wide = jnp.concatenate([vals, vals], axis=1)
    row = iota(wide.shape, 0)
    return jnp.where(row % Q == iota(wide.shape, 1) // DEAD, wide, 0.0).astype(BF16)


def to_slab(ref, width):
    rows = iota((SLAB, width), 0)
    out = jnp.zeros((SLAB, width), F32)
    for r in range(3):
        for q in range(Q):
            piece = ref[r : r + 1, q * width : (q + 1) * width].astype(F32)
            out = jnp.where(rows == Q * r + q, piece, out)
    return out


def kernel(
    res_in, err_in, enc_in, dec_in, mask_in,
    dgrad_ref, egrad_ref, pick_ref,
    e4, w4, e4t, w4t, ybuf, rbuf, gbuf, obuf, osib, s1, xrecv, s2, yrecv, ghost, aexp, pexp, zsend, zhalf, zrel, zrecv, zall,
    res_ref, err_ref, enc_ref, dec_ref, mask_ref, l_s, t_s,
    w_s, w_r, gy_s, gy_r, gx_s, gx_r, gs_s, gs_r, os_s, os_r, ox_s, ox_r, oy_s, oy_r,
    h_s, h_r, z_s, z_r, a_s, a_r, f_s, f_r,
):
    width = e4.shape[1]
    loads = [
        pltpu.make_async_copy(src, dst, l_s.at[i])
        for i, (src, dst) in enumerate(
            ((res_in, res_ref), (mask_in, mask_ref), (enc_in, enc_ref), (dec_in, dec_ref), (err_in, err_ref))
        )
    ]
    for load in loads:
        load.start()
    feats = width * Q
    plane = NX * NY
    dp, lat = lax.axis_index("dp"), lax.axis_index("latent")
    c, zhi = lax.rem(dp, 2), lax.div(dp, 2)
    zlo, inplane = lax.div(lat, plane), lax.rem(lat, plane)
    y, x = lax.div(inplane, NX), lax.rem(inplane, NX)
    z = zhi * 2 + zlo
    o = 1 - c
    own = zlo == c

    def at(xx, yy, zz, cc):
        return (lax.div(zz, 2) * 2 + cc, lax.rem(zz, 2) * plane + yy * NX + xx)

    def yof(d):
        return at(x, lax.rem(y + d, NY), z, c)

    def xof(d):
        return at(lax.rem(x + d, NX), y, z, c)

    def zof(d):
        return at(x, y, lax.rem(z + d, NZ), c)

    sibling = at(x, y, z, o)

    def remote(src, dst, send, recv, dev):
        return pltpu.make_async_remote_copy(
            src_ref=src, dst_ref=dst, send_sem=send, recv_sem=recv, device_id=dev, device_id_type=MESH
        )

    def block(cc, xx):
        return pl.ds(cc * NX + xx, 1)

    xorder = [d for d in (1, 3, 2) if d < NX]
    pending = []

    def go(copy):
        copy.start()
        pending.append(copy)
        return copy

    barrier = pltpu.get_barrier_semaphore()
    partners = [yof(d) for d in range(1, NY)] + [xof(d) for d in range(1, NX)] + [zof(d) for d in (1, 2, NZ - 2, NZ - 1)] + [sibling]
    for dev in partners:
        pl.semaphore_signal(barrier, inc=1, device_id=dev, device_id_type=MESH)
    pl.semaphore_wait(barrier, len(partners))

    cut = width // 256 * 128 + (128 if width % 256 else 0) if width > 128 else 128
    chunks = [pl.ds(0, cut)] + ([pl.ds(cut, width - cut)] if width > cut else [])

    line = NY * REAL
    slot, place = iota((line, NY * SLAB), 0), iota((line, NY * SLAB), 1)
    pack = jnp.where(slot // REAL * SLAB + slot % REAL == place, 1.0, 0.0).astype(BF16)

    def gather_y(k):
        copies = []
        for h, cols in enumerate(chunks):
            part = ybuf.at[k, pl.ds(y, 1), :, cols]
            copies.append(
                [go(remote(part, part, gy_s.at[k, h, d - 1], gy_r.at[k, h, d - 1], yof(d))) for d in range(1, NY)]
            )
        return copies

    def gather_x(buf, k, ycopies):
        xcopies, forward = [], []
        for h, cols in enumerate(chunks):
            for copy in ycopies[h]:
                copy.wait_recv()
            slabs = ybuf[k, :, :, cols].reshape(NY * SLAB, -1)
            buf[block(c, x), :, cols] = dot_nn(pack, slabs).astype(BF16)[None]
            mine = buf.at[block(c, x), :, cols]
            xcopies.append(
                {d: go(remote(mine, mine, gx_s.at[k, h, d - 1], gx_r.at[k, h, d - 1], xof(d))) for d in xorder}
            )
            forward.append({0: go(remote(mine, mine, gs_s.at[k, h, 0], gs_r.at[k, h, 0], sibling))})
        return xcopies, forward

    def gather_next(buf, k, xcopies, forward, d, h):
        xcopies[h][d].wait_recv()
        got = buf.at[block(c, lax.rem(x + NX - d, NX)), :, chunks[h]]
        forward[h][d] = go(remote(got, got, gs_s.at[k, h, d], gs_r.at[k, h, d], sibling))

    loads[0].wait()
    ybuf[0, pl.ds(y, 1)] = to_slab(res_ref, width).astype(BF16)[None]
    ycopies = gather_y(0)

    loads[1].wait()
    mask = mask_ref[...].astype(F32)
    upper = (iota((128, 128), 0) <= iota((128, 128), 1)).astype(BF16)
    rank = dot_nn(jnp.broadcast_to(mask, (16, 128)).astype(BF16), upper)[0:1]
    order = iota((DEAD, 128), 0).astype(F32) + 1.0
    pick = jnp.where((order == rank) & (mask > 0.5), 1.0, 0.0).astype(BF16)
    pick_ref[...] = pick

    weights = [
        remote(ref, ref, w_s.at[i], w_r.at[i], at(x, y, z + 1 - 2 * zlo, c)) for i, ref in enumerate((e4, w4))
    ]

    loads[2].wait()
    loads[3].wait()
    loads[4].wait()

    @pl.when(own)
    def _():
        for q in range(Q):
            e4[pl.ds(q * DEAD, DEAD), :] = dot_nt(pick, enc_ref[q * width : (q + 1) * width, :]).astype(BF16)
        weights[0].start()
        for q in range(Q):
            w4[pl.ds(q * DEAD, DEAD), :] = dot_nn(pick, dec_ref[:, q * width : (q + 1) * width]).astype(BF16)
        weights[1].start()

    xcopies, forward = gather_x(rbuf, 0, ycopies)

    @pl.when(jnp.logical_not(own))
    def _():
        weights[0].wait_recv()
        weights[1].wait_recv()

    e4t[...] = e4[...].T
    w4t[...] = w4[...].T

    def run_block(cc, xx):
        b = cc * NX + xx
        here = pl.ds(pl.multiple_of(b * line, 32 if line % 32 == 0 else 8), line)
        pre = fold(dot_nn(rbuf[b], e4t[...]))
        val = jnp.exp(pre)
        ghost[here, :] = val
        spread = unfold(val)
        aexp[here, :] = spread
        obuf[b] = dot_nn(spread, w4[...]).astype(BF16)

    ocopies, oxcopies = {}, {}

    def add_sibling(d):
        xx = lax.rem(x + NX - d, NX)
        ocopies[d].wait_recv()
        s1[xx] = (obuf[c * NX + xx].astype(F32) + osib[xx].astype(F32)).astype(BF16)
        if d:
            t = NX - d
            oxcopies[t] = go(
                remote(s1.at[xx], xrecv.at[t - 1], ox_s.at[t - 1], ox_r.at[t - 1], xof(t))
            )

    order = [0] + xorder
    for i, d in enumerate(order):
        xx = lax.rem(x + NX - d, NX)
        if d:
            for h in range(len(chunks)):
                gather_next(rbuf, 0, xcopies, forward, d, h)
        run_block(c, xx)
        for copies in forward:
            copies[d].wait_recv()
        run_block(o, xx)
        ocopies[d] = go(remote(obuf.at[o * NX + xx], osib.at[xx], os_s.at[d], os_r.at[d], sibling))
        if i > 1:
            add_sibling(order[i - 1])
    add_sibling(order[-1])
    add_sibling(0)

    for d in xorder:
        oxcopies[d].wait_recv()
    total = s1[x].astype(F32)
    for t in range(NX - 1):
        total += xrecv[t].astype(F32)
    s2[...] = dot_tn(pack, total.astype(BF16)).astype(BF16).reshape(NY, SLAB, width)
    oycopies = []
    for d in range(1, NY):
        oycopies.append(
            go(remote(s2.at[lax.rem(y + d, NY)], yrecv.at[d - 1], oy_s.at[d - 1], oy_r.at[d - 1], yof(d)))
        )
    out = s2[y].astype(F32)
    for d in range(1, NY):
        oycopies[d - 1].wait_recv()
        out += yrecv[d - 1].astype(F32)

    def rms(v):
        squares = jnp.broadcast_to(jnp.sum(v * v, axis=1, keepdims=True), (SLAB, 128))
        return jnp.sqrt(sum_quads(squares) / feats + EPS)[:, 0:1]

    err = to_slab(err_ref, width)
    err_rms = rms(err)
    scale = err_rms / (2.0 * rms(out))
    ybuf[1, pl.ds(y, 1)] = (scale * (scale * out - err) / err_rms).astype(BF16)[None]
    ycopies = gather_y(1)
    xcopies, forward = gather_x(gbuf, 1, ycopies)

    def gather_chunk(h):
        for d in xorder:
            gather_next(gbuf, 1, xcopies, forward, d, h)
        for d in order:
            forward[h][d].wait_recv()

    tokens = 2 * plane * REAL
    factor = 1.0 / math.sqrt(NZ * 2 * plane * 3)
    to_left = lax.rem(zhi + Q - 1, Q)
    to_right = lax.rem(zhi + 1, Q)
    across = lax.rem(zhi + 2, Q)
    right, left = zof(2), zof(NZ - 2)
    top, low = pl.ds(0, DEAD // 2), pl.ds(DEAD // 2, DEAD // 2)
    half = Q // 2

    def halves(kind, h):
        copies = []
        for i, d in enumerate((1, NZ - 1)):
            at_rows = pl.ds(kind * Q + i * half, half)
            copies.append(
                remote(
                    zsend.at[at_rows, :, chunks[h]], zhalf.at[at_rows, :, chunks[h]],
                    h_s.at[kind, h, i], h_r.at[kind, h, i], zof(d),
                )
            )
        return copies

    def gradient(lhs, rhs, kind, h):
        part = (dot_tn(lhs[...], rhs[:, :, chunks[h]].reshape(tokens, -1)) * factor).astype(BF16)
        for q in range(Q):
            zsend[kind * Q + q, :, chunks[h]] = part[q * DEAD : (q + 1) * DEAD]

        @pl.when(jnp.logical_not(own))
        def _():
            for copy in halves(kind, h):
                copy.start()

    def z_copy(kind, i):
        k = kind * Q
        pairs = (
            (zsend.at[k + across, top], zrel.at[kind, 0], right),
            (zsend.at[k + across, low], zrel.at[kind, 1], left),
            (zsend.at[k + to_right, low], zrecv.at[kind, 0, low], right),
            (zsend.at[k + to_left, top], zrecv.at[kind, 1, top], left),
            (zsend.at[k + to_right, top], zrecv.at[kind, 0, top], right),
            (zsend.at[k + to_left, low], zrecv.at[kind, 1, low], left),
        )
        src, dst, dev = pairs[i]
        return remote(src, dst, z_s.at[kind, i], z_r.at[kind, i], dev)

    def a_copy(kind, i):
        sent = (
            (zhi, top, right), (zhi, low, left), (zhi, low, right), (zhi, top, left),
            (to_left, top, right), (to_right, low, left),
        )
        p, rows, dev = sent[i]
        part = zall.at[kind * Q + p, rows]
        return remote(part, part, a_s.at[kind, i], a_r.at[kind, i], dev)

    def hand(kind, i):
        piece = zall.at[kind * Q + (zhi, to_left, to_right, across)[i]]
        return remote(piece, piece, f_s.at[kind, i], f_r.at[kind, i], sibling)

    def store(kind, q):
        cols = pl.ds(q * width, width)
        return pltpu.make_async_copy(zall.at[kind * Q + q], (dgrad_ref, egrad_ref)[kind].at[:, cols], t_s.at[kind, q])

    def add_halves(kind):
        for h in range(len(chunks)):
            for copy in halves(kind, h):
                copy.wait_recv()
        for p, sends in ((across, (0, 1)), (to_right, (2,)), (to_left, (3,)), (zhi, ())):
            p = kind * Q + p
            zsend[p] = (zsend[p].astype(F32) + zhalf[p].astype(F32)).astype(BF16)
            for i in sends:
                z_copy(kind, i).start()

    def relay(kind):
        for i, p, rows in ((0, to_right, top), (1, to_left, low)):
            z_copy(kind, i).wait_recv()
            p = kind * Q + p
            zsend[p, rows] = (zsend[p, rows].astype(F32) + zrel[kind, i].astype(F32)).astype(BF16)
            z_copy(kind, 4 + i).start()

    def add_members(kind):
        for i in range(2, 6):
            z_copy(kind, i).wait_recv()
        p = kind * Q + zhi
        zall[p] = (zsend[p].astype(F32) + zrecv[kind, 0].astype(F32) + zrecv[kind, 1].astype(F32)).astype(BF16)
        for i in range(4):
            a_copy(kind, i).start()
        hand(kind, 0).start()

    def share(kind):
        for i in range(2):
            a_copy(kind, i).wait_recv()
            a_copy(kind, 4 + i).start()
        for i in range(2):
            a_copy(kind, 2 + i).wait_recv()
            hand(kind, 1 + i).start()

    def finish(kind):
        for i in range(4, 6):
            a_copy(kind, i).wait_recv()
        hand(kind, 3).start()
        for q in range(Q):
            store(kind, q).start()

    for h in range(len(chunks)):
        gather_chunk(h)
        gradient(aexp, gbuf, 0, h)
    for b in range(2 * NX):
        here = pl.ds(b * line, line)
        back = fold(dot_nn(gbuf[b], w4t[...]))
        pexp[here, :] = unfold(back * ghost[here, :])

    @pl.when(own)
    def _():
        add_halves(0)

    for h in range(len(chunks)):
        gradient(pexp, rbuf, 1, h)

    @pl.when(own)
    def _():
        relay(0)
        add_halves(1)
        add_members(0)
        relay(1)
        share(0)
        add_members(1)
        finish(0)
        share(1)
        finish(1)

    @pl.when(jnp.logical_not(own))
    def _():
        for kind in range(2):
            for i in range(Q):
                hand(kind, i).wait_recv()
            for q in range(Q):
                store(kind, q).start()

    for kind in range(2):
        for q in range(Q):
            store(kind, q).wait()

    @pl.when(own)
    def _():
        for copy in weights:
            copy.wait_send()
        for kind in range(2):
            for i in range(6):
                z_copy(kind, i).wait_send()
                a_copy(kind, i).wait_send()
            for i in range(Q):
                hand(kind, i).wait_send()

    @pl.when(jnp.logical_not(own))
    def _():
        for kind in range(2):
            for h in range(len(chunks)):
                for copy in halves(kind, h):
                    copy.wait_send()

    for copy in pending:
        copy.wait_send()


def body(residual, errors, enc_weight, dec_weight, dead_mask):
    feats = residual.shape[1]
    width = feats // Q
    line = NY * REAL
    dma = pltpu.SemaphoreType.DMA
    vmem = pl.BlockSpec(memory_space=pltpu.VMEM)

    def held(n):
        return pltpu.VMEM((n, line, width), BF16)

    dgrad, egrad, pick = pl.pallas_call(
        kernel,
        out_shape=(
            jax.ShapeDtypeStruct((DEAD, feats), BF16),
            jax.ShapeDtypeStruct((DEAD, feats), BF16),
            jax.ShapeDtypeStruct((DEAD, 128), BF16),
        ),
        in_specs=[pl.BlockSpec(memory_space=pl.ANY)] * 5,
        out_specs=(pl.BlockSpec(memory_space=pl.ANY),) * 2 + (vmem,),
        scratch_shapes=[
            pltpu.VMEM((Q * DEAD, width), BF16),
            pltpu.VMEM((Q * DEAD, width), BF16),
            pltpu.VMEM((width, Q * DEAD), BF16),
            pltpu.VMEM((width, Q * DEAD), BF16),
            pltpu.VMEM((2, NY, SLAB, width), BF16),
            held(2 * NX),
            held(2 * NX),
            held(2 * NX),
            held(NX),
            held(NX),
            held(NX - 1),
            pltpu.VMEM((NY, SLAB, width), BF16),
            pltpu.VMEM((NY - 1, SLAB, width), BF16),
            pltpu.VMEM((2 * NX * line, 2 * DEAD), F32),
            pltpu.VMEM((2 * NX * line, Q * DEAD), BF16),
            pltpu.VMEM((2 * NX * line, Q * DEAD), BF16),
            pltpu.VMEM((2 * Q, DEAD, width), BF16),
            pltpu.VMEM((2 * Q, DEAD, width), BF16),
            pltpu.VMEM((2, 2, DEAD // 2, width), BF16),
            pltpu.VMEM((2, 2, DEAD, width), BF16),
            pltpu.VMEM((2 * Q, DEAD, width), BF16),
            pltpu.VMEM(residual.shape, BF16),
            pltpu.VMEM(errors.shape, BF16),
            pltpu.VMEM(enc_weight.shape, BF16),
            pltpu.VMEM(dec_weight.shape, BF16),
            pltpu.VMEM((1, dead_mask.shape[0]), jnp.int32),
            dma((5,)),
            dma((2, Q)),
            dma((2,)), dma((2,)),
            dma((2, 2, NY - 1)), dma((2, 2, NY - 1)),
            dma((2, 2, NX - 1)), dma((2, 2, NX - 1)),
            dma((2, 2, NX)), dma((2, 2, NX)),
            dma((NX,)), dma((NX,)),
            dma((NX - 1,)), dma((NX - 1,)),
            dma((NY - 1,)), dma((NY - 1,)),
            dma((2, 2, 2)), dma((2, 2, 2)),
            dma((2, 6)), dma((2, 6)),
            dma((2, 6)), dma((2, 6)),
            dma((2, Q)), dma((2, Q)),
        ],
        compiler_params=pltpu.CompilerParams(
            collective_id=0, has_side_effects=True, vmem_limit_bytes=56 * 1024 * 1024
        ),
    )(residual, errors, enc_weight, dec_weight, dead_mask.reshape(1, -1))
    enc_grad = dot_tn(egrad, pick).astype(BF16)
    dec_grad = dot_tn(pick, dgrad).astype(BF16)
    return enc_grad, dec_grad


def solution(mesh):
    return jax.shard_map(
        body,
        mesh=mesh,
        in_specs=(
            P(("dp", "latent"), None),
            P(("dp", "latent"), None),
            P(None, "latent"),
            P("latent", None),
            P("latent"),
        ),
        out_specs=(P(None, "latent"), P("latent", None)),
        check_vma=False,
    )
```

```python
import math

import jax
import jax.numpy as jnp
from jax import lax
from jax.experimental import pallas as pl
from jax.experimental.pallas import tpu as pltpu
from jax.sharding import PartitionSpec as P

NX, NY, NZ = 4, 8, 8
DEAD = 64
Q = 4
SLAB = 16
REAL = 3 * Q
EPS = 1e-06
MESH = pl.DeviceIdType.MESH
F32, BF16 = jnp.float32, jnp.bfloat16


def dot_nt(a, b):
    return lax.dot_general(a, b, (((1,), (1,)), ((), ())), preferred_element_type=F32)


def dot_nn(a, b):
    return lax.dot_general(a, b, (((1,), (0,)), ((), ())), preferred_element_type=F32)


def dot_tn(a, b):
    return lax.dot_general(a, b, (((0,), (0,)), ((), ())), preferred_element_type=F32)


def iota(shape, dim):
    return lax.broadcasted_iota(jnp.int32, shape, dim)


def sum_quads(v):
    n = v.shape[0]
    row = iota(v.shape, 0)
    v = v + jnp.where(row % 2 == 0, pltpu.roll(v, n - 1, 0), pltpu.roll(v, 1, 0))
    return v + jnp.where(row % 4 < 2, pltpu.roll(v, n - 2, 0), pltpu.roll(v, 2, 0))


def fold(prod):
    same = iota(prod.shape, 0) % Q == iota(prod.shape, 1) // DEAD
    prod = jnp.where(same, prod, 0.0)
    half = 2 * DEAD
    pair = prod[:, :half] + prod[:, half:]
    return sum_quads(pair + pltpu.roll(pair, DEAD, 1))


def unfold(vals):
    wide = jnp.concatenate([vals, vals], axis=1)
    row = iota(wide.shape, 0)
    return jnp.where(row % Q == iota(wide.shape, 1) // DEAD, wide, 0.0).astype(BF16)


def to_slab(ref, width):
    rows = iota((SLAB, width), 0)
    out = jnp.zeros((SLAB, width), F32)
    for r in range(3):
        for q in range(Q):
            piece = ref[r : r + 1, q * width : (q + 1) * width].astype(F32)
            out = jnp.where(rows == Q * r + q, piece, out)
    return out


def kernel(
    res_in, err_in, enc_in, dec_in, mask_in,
    dgrad_ref, egrad_ref, pick_ref,
    e4, w4, e4t, w4t, ybuf, rbuf, gbuf, obuf, osib, s1, xrecv, s2, yrecv, ghost, aexp, pexp, zsend, zhalf, zrel, zrecv, zall,
    res_ref, err_ref, enc_ref, dec_ref, mask_ref, l_s, t_s,
    w_s, w_r, gy_s, gy_r, gx_s, gx_r, gs_s, gs_r, os_s, os_r, ox_s, ox_r, oy_s, oy_r,
    h_s, h_r, z_s, z_r, a_s, a_r, f_s, f_r,
):
    width = e4.shape[1]
    loads = [
        pltpu.make_async_copy(src, dst, l_s.at[i])
        for i, (src, dst) in enumerate(
            ((res_in, res_ref), (mask_in, mask_ref), (enc_in, enc_ref), (dec_in, dec_ref), (err_in, err_ref))
        )
    ]
    for load in loads:
        load.start()
    feats = width * Q
    plane = NX * NY
    dp, lat = lax.axis_index("dp"), lax.axis_index("latent")
    c, zhi = lax.rem(dp, 2), lax.div(dp, 2)
    zlo, inplane = lax.div(lat, plane), lax.rem(lat, plane)
    y, x = lax.div(inplane, NX), lax.rem(inplane, NX)
    z = zhi * 2 + zlo
    o = 1 - c
    own = zlo == c

    def at(xx, yy, zz, cc):
        return (lax.div(zz, 2) * 2 + cc, lax.rem(zz, 2) * plane + yy * NX + xx)

    def yof(d):
        return at(x, lax.rem(y + d, NY), z, c)

    def xof(d):
        return at(lax.rem(x + d, NX), y, z, c)

    def zof(d):
        return at(x, y, lax.rem(z + d, NZ), c)

    sibling = at(x, y, z, o)

    def remote(src, dst, send, recv, dev):
        return pltpu.make_async_remote_copy(
            src_ref=src, dst_ref=dst, send_sem=send, recv_sem=recv, device_id=dev, device_id_type=MESH
        )

    def block(cc, xx):
        return pl.ds(cc * NX + xx, 1)

    xorder = [d for d in (1, 3, 2) if d < NX]
    pending = []

    def go(copy):
        copy.start()
        pending.append(copy)
        return copy

    barrier = pltpu.get_barrier_semaphore()
    partners = [yof(d) for d in range(1, NY)] + [xof(d) for d in range(1, NX)] + [zof(d) for d in (1, 2, NZ - 2, NZ - 1)] + [sibling]
    for dev in partners:
        pl.semaphore_signal(barrier, inc=1, device_id=dev, device_id_type=MESH)
    pl.semaphore_wait(barrier, len(partners))

    cut = max(width // 256 * 128, 128)
    chunks = [pl.ds(0, cut)] + ([pl.ds(cut, width - cut)] if width > cut else [])

    line = NY * REAL
    slot, place = iota((line, NY * SLAB), 0), iota((line, NY * SLAB), 1)
    pack = jnp.where(slot // REAL * SLAB + slot % REAL == place, 1.0, 0.0).astype(BF16)

    def gather_y(k):
        copies = []
        for h, cols in enumerate(chunks):
            part = ybuf.at[k, pl.ds(y, 1), :, cols]
            copies.append(
                [go(remote(part, part, gy_s.at[k, h, d - 1], gy_r.at[k, h, d - 1], yof(d))) for d in range(1, NY)]
            )
        return copies

    def gather_x(buf, k, ycopies):
        xcopies, forward = [], []
        for h, cols in enumerate(chunks):
            for copy in ycopies[h]:
                copy.wait_recv()
            slabs = ybuf[k, :, :, cols].reshape(NY * SLAB, -1)
            buf[block(c, x), :, cols] = dot_nn(pack, slabs).astype(BF16)[None]
            mine = buf.at[block(c, x), :, cols]
            xcopies.append(
                {d: go(remote(mine, mine, gx_s.at[k, h, d - 1], gx_r.at[k, h, d - 1], xof(d))) for d in xorder}
            )
            forward.append({0: go(remote(mine, mine, gs_s.at[k, h, 0], gs_r.at[k, h, 0], sibling))})
        return xcopies, forward

    def gather_next(buf, k, xcopies, forward, d, h):
        xcopies[h][d].wait_recv()
        got = buf.at[block(c, lax.rem(x + NX - d, NX)), :, chunks[h]]
        forward[h][d] = go(remote(got, got, gs_s.at[k, h, d], gs_r.at[k, h, d], sibling))

    loads[0].wait()
    ybuf[0, pl.ds(y, 1)] = to_slab(res_ref, width).astype(BF16)[None]
    ycopies = gather_y(0)

    loads[1].wait()
    mask = mask_ref[...].astype(F32)
    upper = (iota((128, 128), 0) <= iota((128, 128), 1)).astype(BF16)
    rank = dot_nn(jnp.broadcast_to(mask, (16, 128)).astype(BF16), upper)[0:1]
    order = iota((DEAD, 128), 0).astype(F32) + 1.0
    pick = jnp.where((order == rank) & (mask > 0.5), 1.0, 0.0).astype(BF16)
    pick_ref[...] = pick

    weights = [
        remote(ref, ref, w_s.at[i], w_r.at[i], at(x, y, z + 1 - 2 * zlo, c)) for i, ref in enumerate((e4, w4))
    ]

    loads[2].wait()
    loads[3].wait()
    loads[4].wait()

    @pl.when(own)
    def _():
        for q in range(Q):
            e4[pl.ds(q * DEAD, DEAD), :] = dot_nt(pick, enc_ref[q * width : (q + 1) * width, :]).astype(BF16)
        weights[0].start()
        for q in range(Q):
            w4[pl.ds(q * DEAD, DEAD), :] = dot_nn(pick, dec_ref[:, q * width : (q + 1) * width]).astype(BF16)
        weights[1].start()

    xcopies, forward = gather_x(rbuf, 0, ycopies)

    @pl.when(jnp.logical_not(own))
    def _():
        weights[0].wait_recv()
        weights[1].wait_recv()

    e4t[...] = e4[...].T
    w4t[...] = w4[...].T

    def run_block(cc, xx):
        b = cc * NX + xx
        here = pl.ds(pl.multiple_of(b * line, 32 if line % 32 == 0 else 8), line)
        pre = fold(dot_nn(rbuf[b], e4t[...]))
        val = jnp.exp(pre)
        ghost[here, :] = val
        spread = unfold(val)
        aexp[here, :] = spread
        obuf[b] = dot_nn(spread, w4[...]).astype(BF16)

    ocopies, oxcopies = {}, {}

    def add_sibling(d):
        xx = lax.rem(x + NX - d, NX)
        ocopies[d].wait_recv()
        s1[xx] = (obuf[c * NX + xx].astype(F32) + osib[xx].astype(F32)).astype(BF16)
        if d:
            t = NX - d
            oxcopies[t] = go(
                remote(s1.at[xx], xrecv.at[t - 1], ox_s.at[t - 1], ox_r.at[t - 1], xof(t))
            )

    order = [0] + xorder
    for i, d in enumerate(order):
        xx = lax.rem(x + NX - d, NX)
        if d:
            for h in range(len(chunks)):
                gather_next(rbuf, 0, xcopies, forward, d, h)
        run_block(c, xx)
        for copies in forward:
            copies[d].wait_recv()
        run_block(o, xx)
        ocopies[d] = go(remote(obuf.at[o * NX + xx], osib.at[xx], os_s.at[d], os_r.at[d], sibling))
        if i > 1:
            add_sibling(order[i - 1])
    add_sibling(order[-1])
    add_sibling(0)

    for d in xorder:
        oxcopies[d].wait_recv()
    total = s1[x].astype(F32)
    for t in range(NX - 1):
        total += xrecv[t].astype(F32)
    s2[...] = dot_tn(pack, total.astype(BF16)).astype(BF16).reshape(NY, SLAB, width)
    oycopies = []
    for d in range(1, NY):
        oycopies.append(
            go(remote(s2.at[lax.rem(y + d, NY)], yrecv.at[d - 1], oy_s.at[d - 1], oy_r.at[d - 1], yof(d)))
        )
    out = s2[y].astype(F32)
    for d in range(1, NY):
        oycopies[d - 1].wait_recv()
        out += yrecv[d - 1].astype(F32)

    def rms(v):
        squares = jnp.broadcast_to(jnp.sum(v * v, axis=1, keepdims=True), (SLAB, 128))
        return jnp.sqrt(sum_quads(squares) / feats + EPS)[:, 0:1]

    err = to_slab(err_ref, width)
    err_rms = rms(err)
    scale = err_rms / (2.0 * rms(out))
    ybuf[1, pl.ds(y, 1)] = (scale * (scale * out - err) / err_rms).astype(BF16)[None]
    ycopies = gather_y(1)
    xcopies, forward = gather_x(gbuf, 1, ycopies)

    def gather_chunk(h):
        for d in xorder:
            gather_next(gbuf, 1, xcopies, forward, d, h)
        for d in order:
            forward[h][d].wait_recv()

    tokens = 2 * plane * REAL
    factor = 1.0 / math.sqrt(NZ * 2 * plane * 3)
    to_left = lax.rem(zhi + Q - 1, Q)
    to_right = lax.rem(zhi + 1, Q)
    across = lax.rem(zhi + 2, Q)
    right, left = zof(2), zof(NZ - 2)
    top, low = pl.ds(0, DEAD // 2), pl.ds(DEAD // 2, DEAD // 2)
    half = Q // 2

    def halves(kind, h):
        copies = []
        for i, d in enumerate((1, NZ - 1)):
            at_rows = pl.ds(kind * Q + i * half, half)
            copies.append(
                remote(
                    zsend.at[at_rows, :, chunks[h]], zhalf.at[at_rows, :, chunks[h]],
                    h_s.at[kind, h, i], h_r.at[kind, h, i], zof(d),
                )
            )
        return copies

    def gradient(lhs, rhs, kind, h):
        part = (dot_tn(lhs[...], rhs[:, :, chunks[h]].reshape(tokens, -1)) * factor).astype(BF16)
        for q in range(Q):
            zsend[kind * Q + q, :, chunks[h]] = part[q * DEAD : (q + 1) * DEAD]

        @pl.when(jnp.logical_not(own))
        def _():
            for copy in halves(kind, h):
                copy.start()

    def z_copy(kind, i):
        k = kind * Q
        pairs = (
            (zsend.at[k + across, top], zrel.at[kind, 0], right),
            (zsend.at[k + across, low], zrel.at[kind, 1], left),
            (zsend.at[k + to_right, low], zrecv.at[kind, 0, low], right),
            (zsend.at[k + to_left, top], zrecv.at[kind, 1, top], left),
            (zsend.at[k + to_right, top], zrecv.at[kind, 0, top], right),
            (zsend.at[k + to_left, low], zrecv.at[kind, 1, low], left),
        )
        src, dst, dev = pairs[i]
        return remote(src, dst, z_s.at[kind, i], z_r.at[kind, i], dev)

    def a_copy(kind, i):
        sent = (
            (zhi, top, right), (zhi, low, left), (zhi, low, right), (zhi, top, left),
            (to_left, top, right), (to_right, low, left),
        )
        p, rows, dev = sent[i]
        part = zall.at[kind * Q + p, rows]
        return remote(part, part, a_s.at[kind, i], a_r.at[kind, i], dev)

    def hand(kind, i):
        piece = zall.at[kind * Q + (zhi, to_left, to_right, across)[i]]
        return remote(piece, piece, f_s.at[kind, i], f_r.at[kind, i], sibling)

    def store(kind, q):
        cols = pl.ds(q * width, width)
        return pltpu.make_async_copy(zall.at[kind * Q + q], (dgrad_ref, egrad_ref)[kind].at[:, cols], t_s.at[kind, q])

    def add_halves(kind):
        for h in range(len(chunks)):
            for copy in halves(kind, h):
                copy.wait_recv()
        for p, sends in ((across, (0, 1)), (to_right, (2,)), (to_left, (3,)), (zhi, ())):
            p = kind * Q + p
            zsend[p] = (zsend[p].astype(F32) + zhalf[p].astype(F32)).astype(BF16)
            for i in sends:
                z_copy(kind, i).start()

    def relay(kind):
        for i, p, rows in ((0, to_right, top), (1, to_left, low)):
            z_copy(kind, i).wait_recv()
            p = kind * Q + p
            zsend[p, rows] = (zsend[p, rows].astype(F32) + zrel[kind, i].astype(F32)).astype(BF16)
            z_copy(kind, 4 + i).start()

    def add_members(kind):
        for i in range(2, 6):
            z_copy(kind, i).wait_recv()
        p = kind * Q + zhi
        zall[p] = (zsend[p].astype(F32) + zrecv[kind, 0].astype(F32) + zrecv[kind, 1].astype(F32)).astype(BF16)
        for i in range(4):
            a_copy(kind, i).start()
        hand(kind, 0).start()

    def share(kind):
        for i in range(2):
            a_copy(kind, i).wait_recv()
            a_copy(kind, 4 + i).start()
        for i in range(2):
            a_copy(kind, 2 + i).wait_recv()
            hand(kind, 1 + i).start()

    def finish(kind):
        for i in range(4, 6):
            a_copy(kind, i).wait_recv()
        hand(kind, 3).start()
        for q in range(Q):
            store(kind, q).start()

    for h in range(len(chunks)):
        gather_chunk(h)
        gradient(aexp, gbuf, 0, h)
    for b in range(2 * NX):
        here = pl.ds(b * line, line)
        back = fold(dot_nn(gbuf[b], w4t[...]))
        pexp[here, :] = unfold(back * ghost[here, :])

    @pl.when(own)
    def _():
        add_halves(0)

    for h in range(len(chunks)):
        gradient(pexp, rbuf, 1, h)

    @pl.when(own)
    def _():
        relay(0)
        add_halves(1)
        add_members(0)
        relay(1)
        share(0)
        add_members(1)
        finish(0)
        share(1)
        finish(1)

    @pl.when(jnp.logical_not(own))
    def _():
        for kind in range(2):
            for i in range(Q):
                hand(kind, i).wait_recv()
            for q in range(Q):
                store(kind, q).start()

    for kind in range(2):
        for q in range(Q):
            store(kind, q).wait()

    @pl.when(own)
    def _():
        for copy in weights:
            copy.wait_send()
        for kind in range(2):
            for i in range(6):
                z_copy(kind, i).wait_send()
                a_copy(kind, i).wait_send()
            for i in range(Q):
                hand(kind, i).wait_send()

    @pl.when(jnp.logical_not(own))
    def _():
        for kind in range(2):
            for h in range(len(chunks)):
                for copy in halves(kind, h):
                    copy.wait_send()

    for copy in pending:
        copy.wait_send()


def body(residual, errors, enc_weight, dec_weight, dead_mask):
    feats = residual.shape[1]
    width = feats // Q
    line = NY * REAL
    dma = pltpu.SemaphoreType.DMA
    vmem = pl.BlockSpec(memory_space=pltpu.VMEM)

    def held(n):
        return pltpu.VMEM((n, line, width), BF16)

    dgrad, egrad, pick = pl.pallas_call(
        kernel,
        out_shape=(
            jax.ShapeDtypeStruct((DEAD, feats), BF16),
            jax.ShapeDtypeStruct((DEAD, feats), BF16),
            jax.ShapeDtypeStruct((DEAD, 128), BF16),
        ),
        in_specs=[pl.BlockSpec(memory_space=pl.ANY)] * 5,
        out_specs=(pl.BlockSpec(memory_space=pl.ANY),) * 2 + (vmem,),
        scratch_shapes=[
            pltpu.VMEM((Q * DEAD, width), BF16),
            pltpu.VMEM((Q * DEAD, width), BF16),
            pltpu.VMEM((width, Q * DEAD), BF16),
            pltpu.VMEM((width, Q * DEAD), BF16),
            pltpu.VMEM((2, NY, SLAB, width), BF16),
            held(2 * NX),
            held(2 * NX),
            held(2 * NX),
            held(NX),
            held(NX),
            held(NX - 1),
            pltpu.VMEM((NY, SLAB, width), BF16),
            pltpu.VMEM((NY - 1, SLAB, width), BF16),
            pltpu.VMEM((2 * NX * line, 2 * DEAD), F32),
            pltpu.VMEM((2 * NX * line, Q * DEAD), BF16),
            pltpu.VMEM((2 * NX * line, Q * DEAD), BF16),
            pltpu.VMEM((2 * Q, DEAD, width), BF16),
            pltpu.VMEM((2 * Q, DEAD, width), BF16),
            pltpu.VMEM((2, 2, DEAD // 2, width), BF16),
            pltpu.VMEM((2, 2, DEAD, width), BF16),
            pltpu.VMEM((2 * Q, DEAD, width), BF16),
            pltpu.VMEM(residual.shape, BF16),
            pltpu.VMEM(errors.shape, BF16),
            pltpu.VMEM(enc_weight.shape, BF16),
            pltpu.VMEM(dec_weight.shape, BF16),
            pltpu.VMEM((1, dead_mask.shape[0]), jnp.int32),
            dma((5,)),
            dma((2, Q)),
            dma((2,)), dma((2,)),
            dma((2, 2, NY - 1)), dma((2, 2, NY - 1)),
            dma((2, 2, NX - 1)), dma((2, 2, NX - 1)),
            dma((2, 2, NX)), dma((2, 2, NX)),
            dma((NX,)), dma((NX,)),
            dma((NX - 1,)), dma((NX - 1,)),
            dma((NY - 1,)), dma((NY - 1,)),
            dma((2, 2, 2)), dma((2, 2, 2)),
            dma((2, 6)), dma((2, 6)),
            dma((2, 6)), dma((2, 6)),
            dma((2, Q)), dma((2, Q)),
        ],
        compiler_params=pltpu.CompilerParams(
            collective_id=0, has_side_effects=True, vmem_limit_bytes=56 * 1024 * 1024
        ),
    )(residual, errors, enc_weight, dec_weight, dead_mask.reshape(1, -1))
    enc_grad = dot_tn(egrad, pick).astype(BF16)
    dec_grad = dot_tn(pick, dgrad).astype(BF16)
    return enc_grad, dec_grad


def solution(mesh):
    return jax.shard_map(
        body,
        mesh=mesh,
        in_specs=(
            P(("dp", "latent"), None),
            P(("dp", "latent"), None),
            P(None, "latent"),
            P("latent", None),
            P("latent"),
        ),
        out_specs=(P(None, "latent"), P("latent", None)),
        check_vma=False,
    )
```
